32 devices in a mesh: section: 4 (over y, x), dp: 4 (over z), tensor: 2 (over core).
Axes of the slice: x: 2, y: 2, z: 4, core: 2. Of those that a mesh axis runs over, the one named last changes fastest.
Arguments:
- inputs: bfloat16 [4, 4096, 1024], P('section', 'dp'), may hold values from -6 to 6
- lengths: int32 [4, 4], P('dp'), may hold values from 1 to 512, 1024 in all within a row
- gain_attn: float32 [4, 1024], P('section'), may hold values from 0.25 to 1.75
- w_query: bfloat16 [4, 1024, 1024], P('section', None, 'tensor'), may hold values from -0.1875 to 0.1875
- w_key: bfloat16 [4, 1024, 1024], P('section', None, 'tensor'), may hold values from -0.1875 to 0.1875
- w_value: bfloat16 [4, 1024, 1024], P('section', None, 'tensor'), may hold values from -0.1875 to 0.1875
- w_out: bfloat16 [4, 1024, 1024], P('section', 'tensor'), may hold values from -1.5 to 1.5
- gain_ffn: float32 [4, 1024], P('section'), may hold values from 0.25 to 1.75
- w_gate: bfloat16 [4, 1024, 2816], P('section', None, 'tensor'), may hold values from -0.1875 to 0.1875
- w_up: bfloat16 [4, 1024, 2816], P('section', None, 'tensor'), may hold values from -0.1875 to 0.1875
- w_down: bfloat16 [4, 2816, 1024], P('section', 'tensor'), may hold values from -0.15625 to 0.15625
- cotangent: bfloat16 [4, 4096, 1024], P('section', 'dp'), may hold values from -6 to 6
Outputs:
- result: bfloat16 [4, 4096, 1024], P('section', 'dp')
- grad_input: float32 [4, 4096, 1024], P('section', 'dp')
- grad_gain_attn: float32 [4, 1024], P('section')
- grad_w_query: float32 [4, 1024, 1024], P('section', None, 'tensor')
- grad_w_key: float32 [4, 1024, 1024], P('section', None, 'tensor')
- grad_w_value: float32 [4, 1024, 1024], P('section', None, 'tensor')
- grad_w_out: float32 [4, 1024, 1024], P('section', 'tensor')
- grad_gain_ffn: float32 [4, 1024], P('section')
- grad_w_gate: float32 [4, 1024, 2816], P('section', None, 'tensor')
- grad_w_up: float32 [4, 1024, 2816], P('section', None, 'tensor')
- grad_w_down: float32 [4, 2816, 1024], P('section', 'tensor')
The draws below stay inside these ranges and needn't reach their ends.
Inputs may be any that keep to these rules, and one draw needn't show every extreme that they name: Each row gives the lengths of the 4 sequences of one data group, in order; they sum to 1024, and the longest of every row has exactly 512 tokens.
All inputs are finite; a program needn't handle non-finite values.
Results may differ from the reference program's by a relative error of at most 0.02.
Values may be sent and summed in bfloat16 or wider, within the bound.
No kernel may reach another device: no remote copies, remote signals or barrier semaphores. Data moves between devices by JAX's collectives and lax.ppermute only.
A program may use at most 192 MiB of HBM per device.

```python
import math
import jax
import jax.numpy as jnp
import numpy as np
from jax import lax

D = 1024
HEADS = 16
HD = 64
FF = 2816
TOK_DEV = 1024
NSEQ = 4
TOKENS = 4096
N_SECTION = 4
N_DP = 4
N_TENSOR = 2


def shard_levels(rng, dims, pieces, low, largest):
    def one(dim, shards_of):
        heights = jax.random.uniform(jax.random.fold_in(jax.random.fold_in(rng, 6), dim), (shards_of,), jnp.float32, low / len(pieces), largest / len(pieces))
        return jnp.repeat(jnp.exp(heights), dims[dim] // shards_of).reshape((-1,) + (1,) * (len(dims) - dim - 1))

    level = one(*pieces[0])
    for cut in pieces[1:]:
        level = level * one(*cut)
    return level


def split_up(number_of, total, reach, lean):
    portions = [(1 << 20) // math.isqrt(rank ** lean) + 1 for rank in range(2, number_of + 1)]
    rest, counts = total - reach - (number_of - 1), [1] * (number_of - 1)
    while rest > 0:
        free = [i for i in range(number_of - 1) if counts[i] < reach]
        pool, left = sum([portions[i] for i in free]), rest
        for i in free:
            more = min(reach - counts[i], max(1, left * portions[i] // pool), rest)
            counts[i] = counts[i] + more
            rest = rest - more
    return np.array([reach] + counts)


def ragged_sizes(stream_key, amount, total, limit, lean):
    if amount == 2:
        one = jax.random.randint(stream_key, (), max(1, total - limit), min(limit, total - 1) + 1)
        return jnp.stack([one, total - one])
    sizes = jnp.asarray(split_up(amount, total, limit, lean), jnp.int32)
    twos = (amount - 1) // 2
    donor, sink = sizes[1:1 + 2 * twos:2], sizes[2:2 + 2 * twos:2]
    margin = jnp.minimum(donor - 1, limit - sink)
    moved = jax.random.randint(jax.random.fold_in(stream_key, 1), (twos,), 0, 1 << 20) % (margin + 1)
    sizes = sizes.at[1:1 + 2 * twos:2].set(donor - moved).at[2:2 + 2 * twos:2].set(sink + moved)
    return sizes[jax.random.permutation(jax.random.fold_in(stream_key, 2), amount)]


def noise(stream_key, extent, deviation, limit, cuts=(), kind=jnp.bfloat16):
    level = shard_levels(stream_key, extent, cuts, -0.22, 0.18) if cuts else 1.0
    values = jax.random.normal(stream_key, extent, jnp.float32) * deviation * level
    return jnp.minimum(jnp.maximum(values, -limit), limit).astype(kind)


def setup_inputs(seed: int = 0) -> dict:
    keys = jax.random.split(jax.random.key(seed), 13)
    inputs = noise(keys[0], (N_SECTION, TOKENS, D), 1.0, 6.0, ((0, 4), (1, 4)))
    lengths = jax.vmap(lambda own: ragged_sizes(own, NSEQ, TOK_DEV, TOK_DEV // 2, 0))(jax.random.split(keys[1], N_DP)).reshape((N_DP, NSEQ)).astype(jnp.int32)
    gain_attn = jnp.clip(1.0 + 0.15 * jax.random.normal(keys[2], (N_SECTION, D), jnp.float32), 0.25, 1.75)
    w_query = noise(keys[3], (N_SECTION, D, D), D ** -0.5, 0.1875, ((0, 4), (2, 2)))
    w_key = noise(keys[4], (N_SECTION, D, D), D ** -0.5, 0.1875, ((0, 4), (2, 2)))
    w_value = noise(keys[5], (N_SECTION, D, D), D ** -0.5, 0.1875, ((0, 4), (2, 2)))
    w_out = noise(keys[6], (N_SECTION, D, D), (D // 64) ** -0.5, 1.5, ((0, 4), (1, 2)))
    gain_ffn = jnp.clip(1.0 + 0.15 * jax.random.normal(keys[7], (N_SECTION, D), jnp.float32), 0.25, 1.75)
    w_gate = noise(keys[8], (N_SECTION, D, FF), D ** -0.5, 0.1875, ((0, 4), (2, 2)))
    w_up = noise(keys[9], (N_SECTION, D, FF), D ** -0.5, 0.1875, ((0, 4), (2, 2)))
    w_down = noise(keys[10], (N_SECTION, FF, D), (FF // 2) ** -0.5, 0.15625, ((0, 4), (1, 2)))
    cotangent = noise(keys[11], (N_SECTION, TOKENS, D), 1.0, 6.0, ((0, 4), (1, 4)))
    return {"inputs": inputs, "lengths": lengths, "gain_attn": gain_attn, "w_query": w_query, "w_key": w_key, "w_value": w_value, "w_out": w_out, "gain_ffn": gain_ffn, "w_gate": w_gate, "w_up": w_up, "w_down": w_down, "cotangent": cotangent}


EPSILON = 1e-06
MASKED = -1e+30
PRECISE = lax.Precision.HIGHEST

@jax.custom_vjp
def low(v):
    return lax.optimization_barrier(v.astype(jnp.bfloat16)).astype(jnp.float32)

@jax.custom_vjp
def low_back(v):
    return v

def low_keep(v):
    return (low(v), None)

def low_pass(kept, grad):
    return (grad,)

def back_keep(v):
    return (v, None)

def back_low(kept, grad):
    return (low(grad),)
low.defvjp(low_keep, low_pass)
low_back.defvjp(back_keep, back_low)

def layout(lengths_row):
    seq_ends = jnp.cumsum(lengths_row.astype(jnp.int32)).astype(jnp.int32)
    seq_starts = (seq_ends - lengths_row).astype(jnp.int32)
    places = jnp.arange(TOK_DEV, dtype=jnp.int32)
    segment = lax.optimization_barrier(jnp.sum((places[:, None] >= seq_ends[None, :]).astype(jnp.int32), axis=1))
    seq_slots = jnp.arange(NSEQ, dtype=jnp.int32)
    seq_first = lax.optimization_barrier(jnp.sum(jnp.where(segment[:, None] == seq_slots[None, :], seq_starts[None, :], 0), axis=1)).astype(jnp.int32)
    position = (places - seq_first).astype(jnp.float32)
    inv_freq = 10000.0 ** (-(jnp.arange(HD // 2, dtype=jnp.float32) * 2.0 / HD))
    angles = position[:, None] * inv_freq[None, :]
    rot_cos = jnp.concatenate([jnp.cos(angles), jnp.cos(angles)], axis=1)[:, None, :]
    rot_sin = jnp.concatenate([jnp.sin(angles), jnp.sin(angles)], axis=1)[:, None, :]
    return (segment, rot_cos, rot_sin)

def norm_rows(values, gain):
    return values * lax.rsqrt(lax.optimization_barrier(jnp.mean(values * values, axis=-1, keepdims=True)) + EPSILON) * gain

def turn(values, rot_cos, rot_sin):
    half_dim = values.shape[-1] // 2
    swapped = jnp.concatenate([-values[..., half_dim:], values[..., :half_dim]], axis=-1)
    return values * rot_cos + swapped * rot_sin

def attend(queries, keys_rot, mixed, segment):
    places = jnp.arange(TOK_DEV, dtype=jnp.int32)
    scores = low_back(jnp.einsum('qhd,khd->hqk', queries, keys_rot, precision=PRECISE) * HD ** (-0.5))
    allowed = (segment[:, None] == segment[None, :]) & (places[None, :] <= places[:, None])
    scores = jnp.where(allowed[None], scores, MASKED)
    probs = low(jax.nn.softmax(scores, axis=-1))
    return jnp.einsum('hqk,khd->qhd', probs, mixed, precision=PRECISE)

def attend_item(packed):
    return attend(packed[0], packed[1], packed[2], packed[3])

def reference(inputs, lengths, gain_attn, w_query, w_key, w_value, w_out, gain_ffn, w_gate, w_up, w_down, cotangent):
    segment, rot_cos, rot_sin = jax.vmap(layout)(lengths.astype(jnp.int32))
    stream = inputs.astype(jnp.float32).reshape(N_SECTION, N_DP, TOK_DEV, D)
    n_items = N_SECTION * N_DP
    head_shape = (N_SECTION, N_DP, TOK_DEV, HEADS, HD)
    item_shape = (n_items, TOK_DEV, HEADS, HD)
    segments = jnp.broadcast_to(segment[None], (N_SECTION, N_DP, TOK_DEV)).reshape(n_items, TOK_DEV)

    def forward(stream, gain_attn, w_query, w_key, w_value, w_out, gain_ffn, w_gate, w_up, w_down):
        normed = low(norm_rows(stream, gain_attn[:, None, None, :]))
        query_lin = low_back(jnp.einsum('sgtd,sde->sgte', normed, w_query, precision=PRECISE))
        key_lin = low_back(jnp.einsum('sgtd,sde->sgte', normed, w_key, precision=PRECISE))
        value_lin = low_back(jnp.einsum('sgtd,sde->sgte', normed, w_value, precision=PRECISE))
        queries = low(turn(query_lin.reshape(head_shape), rot_cos[None], rot_sin[None]))
        keys_rot = low(turn(key_lin.reshape(head_shape), rot_cos[None], rot_sin[None]))
        value_first = low(value_lin[0])
        mixed = low(0.5 * value_lin + 0.5 * value_first[None])
        attended = lax.map(jax.checkpoint(attend_item), (queries.reshape(item_shape), keys_rot.reshape(item_shape), mixed.reshape(item_shape), segments))
        heads_out = low(low_back(attended.reshape(N_SECTION, N_DP, TOK_DEV, D)))
        partials = jnp.einsum('sgtnc,sncd->sgtnd', heads_out.reshape(N_SECTION, N_DP, TOK_DEV, N_TENSOR, D // N_TENSOR), w_out.reshape(N_SECTION, N_TENSOR, D // N_TENSOR, D), precision=PRECISE)
        middle = stream + low_back(lax.optimization_barrier(jnp.sum(low(partials), axis=3)))
        normed_ffn = low(norm_rows(middle, gain_ffn[:, None, None, :]))
        gate = low_back(jnp.einsum('sgtd,sdf->sgtf', normed_ffn, w_gate, precision=PRECISE))
        up_proj = low_back(jnp.einsum('sgtd,sdf->sgtf', normed_ffn, w_up, precision=PRECISE))
        hidden = low(jax.nn.silu(gate) * up_proj)
        ffn_parts = jnp.einsum('sgtnf,snfd->sgtnd', hidden.reshape(N_SECTION, N_DP, TOK_DEV, N_TENSOR, FF // N_TENSOR), w_down.reshape(N_SECTION, N_TENSOR, FF // N_TENSOR, D), precision=PRECISE)
        return middle + lax.optimization_barrier(jnp.sum(low(ffn_parts), axis=3))
    params = tuple((item.astype(jnp.float32) for item in (gain_attn, w_query, w_key, w_value, w_out, gain_ffn, w_gate, w_up, w_down)))
    result, pullback = jax.vjp(forward, stream, *params)
    gradients = pullback(cotangent.astype(jnp.float32).reshape(N_SECTION, N_DP, TOK_DEV, D))
    return (result.reshape(N_SECTION, TOKENS, D).astype(jnp.bfloat16), gradients[0].reshape(N_SECTION, TOKENS, D), gradients[1], gradients[2], gradients[3], gradients[4], gradients[5], gradients[6], gradients[7], gradients[8], gradients[9])
```

```python
import jax
import jax.numpy as jnp
from jax import lax
from jax.experimental import pallas as pl
from jax.experimental.pallas import tpu as pltpu
from jax.sharding import PartitionSpec as P

HD = 64
WINDOW = 512
EPSILON = 1e-06
MASKED = -1e30
F32 = jnp.float32
BF16 = jnp.bfloat16
MIB = 1024 * 1024
CHUNK = 256


def dot(left, right):
    return lax.dot_general(left, right, (((1,), (0,)), ((), ())), preferred_element_type=F32)


def dot_nt(left, right):
    return lax.dot_general(left, right, (((1,), (1,)), ((), ())), preferred_element_type=F32)


def dot_tn(left, right):
    return lax.dot_general(left, right, (((0,), (0,)), ((), ())), preferred_element_type=F32)


def call(kernel, grid, ins, outs, args, vmem, scratch=(), into=None):
    into = {o: array for o, array in (into or {}).items() if array is not None}
    ins, args, n = list(ins), list(args), len(args)
    body = kernel
    if into:
        ins += [pl.BlockSpec(memory_space=pl.ANY)] * len(into)
        args += list(into.values())

        def body(*refs):
            kernel(*refs[:n], *refs[n + len(into) :])

    return pl.pallas_call(
        body,
        grid=grid,
        in_specs=ins,
        out_specs=[spec for spec, _, _ in outs],
        out_shape=[jax.ShapeDtypeStruct(shape, dtype) for _, shape, dtype in outs],
        scratch_shapes=list(scratch),
        input_output_aliases={n + j: o for j, o in enumerate(into)},
        compiler_params=pltpu.CompilerParams(vmem_limit_bytes=vmem * MIB),
        cost_estimate=pl.CostEstimate(flops=1, bytes_accessed=1, transcendentals=0),
    )(*args)


def rows(block, width):
    return pl.BlockSpec((block, width), lambda i: (i, 0))


def whole(*shape):
    return pl.BlockSpec(shape, lambda i: (0,) * len(shape))


def columns(height, block, first=0):
    return pl.BlockSpec((height, block), lambda i: (0, i + first))


def value_kernel(x_ref, gain_ref, w_ref, normed_ref, *value_refs):
    x = x_ref[...].astype(F32)
    inv_rms = lax.rsqrt(jnp.mean(x * x, axis=1, keepdims=True) + EPSILON)
    normed = (x * inv_rms * gain_ref[...]).astype(BF16)
    normed_ref[...] = normed
    values = dot(normed, w_ref[...]).astype(BF16)
    cut = values.shape[1] // len(value_refs)
    for j, ref in enumerate(value_refs):
        ref[...] = values[:, j * cut : (j + 1) * cut]


def value_proj(x, gain, w_value):
    tokens, width = x.shape
    half = w_value.shape[1] // 2
    block = 256
    return call(
        value_kernel,
        (tokens // block,),
        [rows(block, width), whole(1, width), whole(width, 2 * half)],
        [(rows(block, width), (tokens, width), BF16)] + [(rows(block, half), (tokens, half), BF16)] * 2,
        (x, gain, w_value),
        60,
    )


def swap_halves(u):
    lane = lax.broadcasted_iota(jnp.int32, u.shape, 1) % HD
    return jnp.where(lane < HD // 2, pltpu.roll(u, 128 - HD // 2, 1), pltpu.roll(u, HD // 2, 1))


def query_key_kernel(n_ref, wq_ref, wk_ref, cos_ref, sin_ref, q_ref, k_ref):
    normed = n_ref[...]
    cos, sin = cos_ref[...], sin_ref[...]
    for w_ref, o_ref in ((wq_ref, q_ref), (wk_ref, k_ref)):
        u = dot(normed, w_ref[...])
        for lo in range(0, u.shape[1], 128):
            part = u[:, lo : lo + 128]
            o_ref[:, lo : lo + 128] = (part * cos + swap_halves(part) * sin).astype(BF16)


def query_key_proj(normed, w_query, w_key, cos, sin):
    tokens, width = normed.shape
    out = w_query.shape[1]
    block = 256
    return call(
        query_key_kernel,
        (tokens // block,),
        [rows(block, width), whole(width, out), whole(width, out), rows(block, 128), rows(block, 128)],
        [(rows(block, out), (tokens, out), BF16), (rows(block, out), (tokens, out), BF16)],
        (normed, w_query, w_key, cos, sin),
        32,
    )


def row_starts(len_ref, first, count):
    place = first + lax.broadcasted_iota(jnp.int32, (count, 1), 0)
    start = jnp.zeros((count, 1), jnp.int32)
    end = 0
    for j in range(len_ref.shape[1]):
        end = end + len_ref[0, j]
        start = jnp.where(place >= end, end, start)
    return place, start


def band(len_ref, first, count):
    low = max(0, first - WINDOW)
    place, start = row_starts(len_ref, first, count)
    col = low + lax.broadcasted_iota(jnp.int32, (count, first + count - low), 1)
    return low, (col >= start) & (col <= place)


def head_masks(count):
    lane = lax.broadcasted_iota(jnp.int32, (count, 2 * HD), 1)
    return lane < HD, lane >= HD


def probs_kernel(len_ref, q_ref, k_ref, probs_ref):
    tokens = q_ref.shape[0]
    block = 256
    for at in range(0, tokens, block):
        low, allowed = band(len_ref, at, block)
        queries = q_ref[at : at + block, :] * BF16(HD**-0.5)
        keys = k_ref[low : at + block, :]
        for h, mask in enumerate(head_masks(block)):
            scores = dot_nt(jnp.where(mask, queries, BF16(0)), keys)
            scores = jnp.where(allowed, scores, MASKED)
            exps = jnp.exp(scores - jnp.max(scores, axis=1, keepdims=True))
            total = jnp.sum(exps, axis=1, keepdims=True)
            probs_ref[h, at : at + block, : at + block - low] = (exps * (1.0 / total)).astype(BF16)


def band_width(tokens):
    return min(tokens, WINDOW + 256)


def probabilities(lengths, queries, keys):
    tokens, width = queries.shape
    pair = columns(tokens, 2 * HD)
    wide = band_width(tokens)
    return call(
        probs_kernel,
        (width // (2 * HD),),
        [pl.BlockSpec(memory_space=pltpu.SMEM), pair, pair],
        [(pl.BlockSpec((2, tokens, wide), lambda i: (i, 0, 0)), (width // HD, tokens, wide), BF16)],
        (lengths, queries, keys),
        40,
    )[0]


def heads_kernel(n_arrived, places, section_ref, *refs):
    probs_ref, own_refs, arrived = refs[0], refs[1:3], refs[3 : 3 + n_arrived]
    w_ref, heads_ref, mixed_ref, part_ref = refs[3 + n_arrived :]
    block = heads_ref.shape[0]
    half = own_refs[0].shape[1]
    step = pl.program_id(0)

    for section, sources in enumerate(places):

        @pl.when((step == 0) & (section_ref[0] == section))
        def _():
            for j, source in enumerate(sources):
                first_ref = own_refs[j] if source is None else arrived[source]
                mixed_ref[:, j * half : (j + 1) * half] = (
                    0.5 * own_refs[j][...].astype(F32) + 0.5 * first_ref[...].astype(F32)
                ).astype(BF16)

    first_mask, _ = head_masks(block)
    for i in range(own_refs[0].shape[0] // block):
        at = i * block
        low = max(0, at - WINDOW)

        @pl.when(step == i)
        def _():
            for pair in range(heads_ref.shape[1] // (2 * HD)):
                lanes = slice(pair * 2 * HD, (pair + 1) * 2 * HD)
                values = mixed_ref[low : at + block, lanes]
                both = [dot(probs_ref[2 * pair + h, :, : at + block - low], values) for h in range(2)]
                heads_ref[:, lanes] = jnp.where(first_mask, both[0], both[1]).astype(BF16)

    part_ref[...] = dot(heads_ref[...], w_ref[...]).astype(BF16)


def heads_proj(section, probs, own, arrived, places, w_out):
    tokens, half = own[0].shape
    width, model = w_out.shape
    n_heads, _, wide = probs.shape
    block = 256
    return call(
        lambda *refs: heads_kernel(len(arrived), places, *refs),
        (tokens // block,),
        [pl.BlockSpec(memory_space=pltpu.SMEM), pl.BlockSpec((n_heads, block, wide), lambda i: (0, i, 0))]
        + [whole(tokens, half)] * (2 + len(arrived))
        + [whole(width, model)],
        [
            (rows(block, width), (tokens, width), BF16),
            (whole(tokens, width), (tokens, width), BF16),
            (rows(block, model), (tokens, model), BF16),
        ],
        (section.astype(jnp.int32)[None], probs, *own, *arrived, w_out),
        40,
    )


def attend_back_kernel(
    q_ref, k_ref, mixed_ref, probs_ref, grad_ref, cos_ref, sin_ref, dq_ref, dk_ref, half_ref, key_acc, value_acc
):
    tokens = q_ref.shape[0]
    block = 256
    key_acc[...] = jnp.zeros_like(key_acc)
    value_acc[...] = jnp.zeros_like(value_acc)

    def turned_back(grads, at, count):
        cos, sin = cos_ref[at : at + count, :], sin_ref[at : at + count, :]
        return (grads * cos - swap_halves(grads) * sin).astype(BF16)

    masks = head_masks(block)
    for at in range(0, tokens, block):
        low = max(0, at - WINDOW)
        queries = q_ref[at : at + block, :] * BF16(HD**-0.5)
        grads = grad_ref[at : at + block, :]
        keys = k_ref[low : at + block, :]
        values = mixed_ref[low : at + block, :]
        parts = []
        for h, mask in enumerate(masks):
            q_head = jnp.where(mask, queries, BF16(0))
            g_head = jnp.where(mask, grads, BF16(0))
            probs_low = probs_ref[h, at : at + block, : at + block - low]
            probs = probs_low.astype(F32)
            grad_probs = dot_nt(g_head, values)
            inner = jnp.sum(probs * grad_probs, axis=1, keepdims=True)
            grad_scores = (probs * (grad_probs - inner)).astype(BF16)
            parts.append(dot(grad_scores, keys))
            key_acc[low : at + block, :] += dot_tn(grad_scores, q_head)
            value_acc[low : at + block, :] += dot_tn(probs_low, g_head)
        grad_query = jnp.where(masks[0], parts[0], parts[1]) * HD**-0.5
        dq_ref[at : at + block, :] = turned_back(grad_query, at, block)
    for at in range(0, tokens, block):
        dk_ref[at : at + block, :] = turned_back(key_acc[at : at + block, :], at, block)
    half_ref[...] = (0.5 * value_acc[...]).astype(BF16)


def attend_back(queries, keys, mixed, probs, grad_heads, cos, sin, first, count, into):
    tokens, width = queries.shape
    pair = columns(tokens, 2 * HD, first)
    wide = probs.shape[2]
    return call(
        attend_back_kernel,
        (count,),
        [pair, pair, pair, pl.BlockSpec((2, tokens, wide), lambda i: (i + first, 0, 0)), pair]
        + [whole(tokens, 128), whole(tokens, 128)],
        [(pair, (tokens, width), BF16)] * 3,
        (queries, keys, mixed, probs, grad_heads, cos, sin),
        40,
        scratch=[pltpu.VMEM((tokens, 2 * HD), F32), pltpu.VMEM((tokens, 2 * HD), F32)],
        into=dict(enumerate(into)),
    )


def units_step(normed, grad_out, wg_ref, wu_ref, wd_ref, hidden_ref, dg_ref, du_ref, stacked_ref):
    gate = dot(normed, wg_ref[...])
    up = dot(normed, wu_ref[...])
    grad_hidden = dot_nt(grad_out, wd_ref[...])
    sig = jax.nn.sigmoid(gate)
    silu = gate * sig
    hidden = (silu * up).astype(BF16)
    hidden_ref[...] = hidden
    dg_ref[...] = (grad_hidden * up * (sig * (1.0 + gate * (1.0 - sig)))).astype(BF16)
    du_ref[...] = (grad_hidden * silu).astype(BF16)
    turned = hidden.T
    height, wide = turned.shape[0], stacked_ref.shape[1]
    for j in range(grad_out.shape[1] // wide):
        stacked_ref[j * height : (j + 1) * height, :] = dot(turned, grad_out[:, j * wide : (j + 1) * wide]).astype(BF16)


def entry_kernel(
    x_ref, own_ref, other_ref, gain_ref, grad_ref, wg_ref, wu_ref, wd_ref,
    middle_ref, normed_ref, turned_ref, hidden_ref, dg_ref, du_ref, gwd_ref,
):
    step = pl.program_id(0)
    block = x_ref.shape[0]
    middle = x_ref[...].astype(F32) + (own_ref[...].astype(F32) + other_ref[...].astype(F32))
    middle_ref[...] = middle
    inv_rms = lax.rsqrt(jnp.mean(middle * middle, axis=1, keepdims=True) + EPSILON)
    normed = (middle * inv_rms * gain_ref[...]).astype(BF16)
    normed_ref[pl.ds(pl.multiple_of(step * block, block), block), :] = normed
    turned_ref[...] = normed.T

    @pl.when(step == pl.num_programs(0) - 1)
    def _():
        units_step(normed_ref[...], grad_ref[...], wg_ref, wu_ref, wd_ref, hidden_ref, dg_ref, du_ref, gwd_ref)


def ffn_kernel(normed_ref, grad_ref, wg_ref, wu_ref, wd_ref, hidden_ref, dg_ref, du_ref, gwd_ref):
    units_step(normed_ref[...], grad_ref[...], wg_ref, wu_ref, wd_ref, hidden_ref, dg_ref, du_ref, gwd_ref)


def entry(x, own, other, gain, grad_out, w_gate, w_up, w_down, units):
    tokens, width = x.shape
    block = 256
    tall = width * units // CHUNK
    first = pl.BlockSpec((width, units), lambda i: (0, 0))
    hidden = (pl.BlockSpec((tokens, units), lambda i: (0, 0)), (tokens, w_gate.shape[1]), BF16)
    return call(
        entry_kernel,
        (tokens // block,),
        [rows(block, width)] * 3
        + [whole(1, width), whole(tokens, width), first, first, pl.BlockSpec((units, width), lambda i: (0, 0))],
        [
            (rows(block, width), (tokens, width), F32),
            (whole(tokens, width), (tokens, width), BF16),
            (columns(width, block), (width, tokens), BF16),
            hidden,
            hidden,
            hidden,
            (whole(tall, CHUNK), (tall, CHUNK), BF16),
        ],
        (x, own, other, gain, grad_out, w_gate, w_up, w_down),
        60,
    )


def ffn(normed, grad_out, w_gate, w_up, w_down, units, number, count, into):
    tokens, width = normed.shape
    tall = width * units // CHUNK
    return call(
        ffn_kernel,
        (count,),
        [whole(tokens, width)] * 2
        + [columns(width, units, number)] * 2
        + [pl.BlockSpec((units, width), lambda i: (i + number, 0))],
        [(columns(tokens, units, number), (tokens, w_gate.shape[1]), BF16)] * 3
        + [(rows(tall, CHUNK), (tall * count, CHUNK), BF16)],
        (normed, grad_out, w_gate, w_up, w_down),
        48,
        into=dict(enumerate(into)),
    )


def weight_grads_kernel(turned_ref, *refs):
    half = len(refs) // 2
    for d_ref, o_ref in zip(refs[:half], refs[half:]):
        o_ref[...] = dot(turned_ref[...], d_ref[...]).astype(BF16)


def weight_grads(turned, grads, units, number):
    width, tokens = turned.shape
    block = 256
    column = pl.BlockSpec((tokens, units), lambda i: (0, number))
    return call(
        weight_grads_kernel,
        (width // block,),
        [rows(block, tokens)] + [column] * len(grads),
        [(rows(block, units), (width, units), BF16)] * len(grads),
        (turned, *grads),
        40,
    )


def stacked_grads_kernel(left_ref, right_ref, out_ref, turned):
    @pl.when(pl.program_id(0) == 0)
    def _():
        turned[...] = left_ref[...].T

    out_ref[...] = dot(turned[...], right_ref[...]).astype(BF16)


def stacked_grads(left, right, number):
    tokens, width = right.shape
    return call(
        stacked_grads_kernel,
        (width // CHUNK,),
        [pl.BlockSpec((tokens, CHUNK), lambda i: (0, number)), columns(tokens, CHUNK)],
        [(rows(CHUNK, CHUNK), (width, CHUNK), BF16)],
        (left, right),
        40,
        scratch=[pltpu.VMEM((CHUNK, tokens), BF16)],
    )[0]


def norm_back_kernel(dn_ref, do_ref, v_ref, gain_ref, base_ref, out_ref, *more):
    grad_normed = dn_ref[...].astype(F32) + do_ref[...].astype(F32)
    values = v_ref[...].astype(F32)
    inv_rms = lax.rsqrt(jnp.mean(values * values, axis=1, keepdims=True) + EPSILON)
    weighted = grad_normed * gain_ref[...]
    inner = jnp.mean(weighted * values, axis=1, keepdims=True)
    out = base_ref[...].astype(F32) + inv_rms * weighted - values * (inv_rms * inv_rms * inv_rms) * inner
    out_ref[...] = out
    gain_grad_ref = more[-1]
    if len(more) > 1:
        more[0][...] = out.astype(BF16)

    @pl.when(pl.program_id(0) == 0)
    def _():
        gain_grad_ref[...] = jnp.zeros_like(gain_grad_ref)

    gain_grad_ref[...] += jnp.sum(grad_normed * values * inv_rms, axis=0, keepdims=True)


def norm_back(own, other, values, gain, base, low):
    tokens, width = own.shape
    block = 256
    outs = [(rows(block, width), (tokens, width), F32)]
    if low:
        outs.append((rows(block, width), (tokens, width), BF16))
    outs.append((whole(1, width), (1, width), F32))
    return call(
        norm_back_kernel,
        (tokens // block,),
        [rows(block, width)] * 3 + [whole(1, width), rows(block, width)],
        outs,
        (own, other, values, gain, base),
        40,
    )


def tie(*values):
    return lax.optimization_barrier(values)


def tick_kernel(names, n_sums, flags_ref, *refs):
    refs = dict(zip(names, refs))

    def add(one, two):
        return (refs[one][...].astype(F32) + refs[two][...].astype(F32)).astype(BF16)

    def put_sum(source):
        value = refs[source][...].astype(F32)
        wide = value.shape[1] // max(n_sums, 1)
        for j in range(n_sums):
            refs[f"sum{j}"][...] = value[:, j * wide : (j + 1) * wide]

    is_left, is_end = flags_ref[0] == 1, flags_ref[1] == 1
    for side, inward, outward in ((is_left, "right", "left"), (jnp.logical_not(is_left), "left", "right")):
        go_in = refs.get("go_" + inward, refs.get("go"))
        go_out = refs.get("go_" + outward, refs.get("go"))

        @pl.when(side & is_end)
        def _():
            if "part" in refs:
                go_in[...] = refs["part"][...]
            if n_sums:
                put_sum("arrived_" + outward)

        @pl.when(side & jnp.logical_not(is_end))
        def _():
            if "old_part" in refs:
                go_in[...] = add("old_part", "arrived_" + inward)
            if "back" in refs:
                go_out[...] = add("gone_" + inward, "arrived_" + outward)
            if n_sums:
                put_sum("gone_" + outward)


def tick_call(flags, inputs, gos, back, sums, into):
    steps = {"part": 1, "arrived_right": 3, "arrived_left": 4, "old_part": 2, "gone_right": 2, "gone_left": 2}
    shape = next(iter(inputs.values())).shape
    block = (256, shape[1])
    ins = [
        pl.BlockSpec(block, lambda i, flags, f=steps[name]: (i * flags[f], 0)) for name in inputs
    ]
    outs = [pl.BlockSpec(block, lambda i, flags: (i, 0)) for _ in gos]
    outs += [pl.BlockSpec(b, lambda i, flags, at=at: at(i)) for b, at, _ in sums]
    shapes = [jax.ShapeDtypeStruct(shape, BF16) for _ in gos] + [jax.ShapeDtypeStruct(s, F32) for _, _, s in sums]
    held = [(j, array) for j, array in enumerate(into) if array is not None]
    n_in = len(inputs)
    names = list(inputs) + list(gos) + [f"sum{j}" for j in range(len(sums))] + (["back"] if back else [])

    def body(flags_ref, *refs):
        tick_kernel(names, len(sums), flags_ref, *refs[:n_in], *refs[n_in + len(held) :], *([None] if back else []))

    return pl.pallas_call(
        body,
        grid_spec=pltpu.PrefetchScalarGridSpec(
            num_scalar_prefetch=1,
            grid=(shape[0] // block[0],),
            in_specs=ins + [pl.BlockSpec(memory_space=pl.ANY)] * len(held),
            out_specs=outs,
        ),
        out_shape=shapes,
        input_output_aliases={1 + n_in + h: len(gos) + j for h, (j, _) in enumerate(held)},
        compiler_params=pltpu.CompilerParams(vmem_limit_bytes=24 * MIB),
        cost_estimate=pl.CostEstimate(flops=1, bytes_accessed=1, transcendentals=0),
    )(flags, *inputs.values(), *[array for _, array in held])


class Line:
    def __init__(self, axis, size, shapes):
        self.axis, self.size, self.shapes = axis, size, shapes
        place = lax.axis_index(axis)
        end, left = (place == 0) | (place == 3), place < 2
        mid = jnp.logical_not(end)
        self.flags = jnp.stack([left, end, mid, jnp.where(left, mid, True), jnp.where(left, True, mid)]).astype(jnp.int32)
        self.parts, self.places = [], []
        self.arrived, self.gone = {}, {}
        self.outs = {name: None for name in shapes}
        self.at = 0
        self.clock = []

    def after(self, *values):
        if not self.clock:
            return values if len(values) > 1 else values[0]
        held = tie(*values, *self.clock)[: len(values)]
        return held if len(values) > 1 else held[0]

    def mark(self, *values):
        self.clock = list(values)

    def push(self, part, *places):
        self.places.append(places)
        self.parts.append(part)

    def tick(self, times=1):
        if self.size != 4:
            return
        for _ in range(times):
            k, n = self.at, len(self.parts)
            self.at += 1
            old = k - 2
            inputs = {}
            if k < n:
                inputs["part"] = self.parts[k]
            if old in self.arrived:
                inputs["arrived_right"], inputs["arrived_left"] = self.arrived[old]
            if not inputs:
                continue
            inputs = dict(zip(inputs, tie(*inputs.values(), *self.clock)))
            if k < n:
                self.parts[k] = inputs["part"]
            halves, totals, done = 0 <= k - 2 < n, 0 <= k - 4 < n, 0 <= k - 6 < n
            if halves:
                inputs["old_part"] = self.parts[old]
            if totals or done:
                inputs["gone_right"], inputs["gone_left"] = self.gone[old]
            right, left = [], []
            for wanted, pairs in ((k < n, ((0, 1), (3, 2))), (halves, ((1, 2), (2, 1))), (totals, ((2, 3), (1, 0)))):
                if wanted:
                    right, left = right + [pairs[0]], left + [pairs[1]]
            inner = k < n or halves
            gos = ["go_right", "go_left"] if inner and totals else ["go"] if inner or totals else []
            places = self.places[k - 6] if done else ()
            if k < 2:
                results = [inputs["part"]]
            else:
                results = tick_call(
                    self.flags,
                    inputs,
                    gos,
                    totals,
                    [(block, at, self.shapes[name]) for name, block, at in places],
                    [self.outs[name] for name, _, _ in places],
                )
            go = results[: len(gos)]
            for (name, _, _), array in zip(places, results[len(gos) :]):
                self.outs[name] = array
            if go:
                self.gone[k] = (go[0], go[-1])
                self.arrived[k] = (lax.ppermute(go[0], self.axis, right), lax.ppermute(go[-1], self.axis, left))
                self.mark(*go)
            else:
                self.mark(*results)

    def finish(self):
        if self.size == 4:
            self.tick(len(self.parts) + 6 - self.at)
            return
        for part, places in zip(self.parts, self.places):
            value = lax.psum(part, self.axis).astype(F32)
            from_col = 0
            for name, block, at in places:
                if self.outs[name] is None:
                    self.outs[name] = jnp.zeros(self.shapes[name], F32)
                for i in range(part.shape[0] // 256):
                    where = tuple(b * o for b, o in zip(block, at(i)))
                    piece = value[i * 256 : (i + 1) * 256, from_col : from_col + block[1]]
                    self.outs[name] = lax.dynamic_update_slice(self.outs[name], piece, where)
                from_col += block[1]


def tables(lengths_row, tokens):
    seqs = lengths_row.shape[0]
    slot = jnp.arange(seqs, dtype=jnp.int32)
    ends = jnp.sum(jnp.where(slot[None, :] <= slot[:, None], lengths_row[None, :], 0), axis=1)
    places = jnp.arange(tokens, dtype=jnp.int32)
    start = jnp.sum(jnp.where(places[:, None] >= ends[None, :], lengths_row[None, :], 0), axis=1)
    position = (places - start).astype(F32)
    inv_freq = 10000.0 ** (-(jnp.arange(HD // 2, dtype=F32) * 2.0 / HD))
    angles = position[:, None] * inv_freq[None, :]
    cos, sin = jnp.cos(angles), jnp.sin(angles)
    return jnp.concatenate([cos] * 4, axis=1), jnp.concatenate([-sin, sin, -sin, sin], axis=1)


def exchange(part, axis):
    return lax.ppermute(part, axis, [(0, 1), (1, 0)])


def shards(sizes, *args):
    (x, lengths, gain_attn, w_query, w_key, w_value, w_out, gain_ffn, w_gate, w_up, w_down, grad_out) = args
    x, w_query, w_key, w_value, w_out, w_gate, w_up, w_down, grad_out = (
        a[0] for a in (x, w_query, w_key, w_value, w_out, w_gate, w_up, w_down, grad_out)
    )
    tokens, width = x.shape
    units = w_gate.shape[1]
    rest = units % CHUNK
    n_sections = sizes["section"]
    section = lax.axis_index("section")
    outputs = {"query": w_query, "key": w_key, "value": w_value, "out": w_out, "gate": w_gate, "up": w_up, "down": w_down}
    shapes = {name: w.shape for name, w in outputs.items()}
    shapes["tail"] = (width, CHUNK)
    line = Line("dp", sizes["dp"], shapes)

    def column(name, number, wide=CHUNK):
        return name, (256, wide), lambda i: (i, number)

    def stacked(name, number):
        return name, (CHUNK, CHUNK), lambda i: (number, i)

    normed, *own = value_proj(x, gain_attn, w_value)

    def send(block, *pairs):
        return lax.ppermute(block, "section", list(pairs))

    relay = n_sections == 4
    if relay:
        one, two = send(own[0], (0, 1)), send(own[1], (0, 2))
    cos, sin = tables(lengths[0], tokens)
    queries, keys = query_key_proj(normed, w_query, w_key, cos, sin)
    if relay:
        one, two, queries = tie(one, two, queries)
        three = send(jnp.where(section == 0, own[1], one), (0, 1), (1, 3))
        four = send(jnp.where(section == 0, own[0], two), (0, 2), (2, 3))
        queries, three_, four_ = queries, three, four
        arrived = [one, two, three, four]
        places = [(None, None), (0, 2), (3, 1), (2, 3)]
    else:
        arrived = [send(half, (0, s)) for s in range(1, n_sections) for half in own]
        places = [(None, None)] + [(2 * s, 2 * s + 1) for s in range(n_sections - 1)]
    probs = probabilities(lengths, queries, keys)
    probs, *arrived = tie(probs, *arrived)
    heads, mixed, part = heads_proj(section, probs, own, arrived, places, w_out)

    weights = (w_gate, w_up, w_down)
    middle, normed_ffn, turned_ffn, *acts, down = entry(
        x, part, exchange(part, "tensor"), gain_ffn, grad_out, *weights, CHUNK
    )
    line.push(down, stacked("down", 0))
    line.tick()

    def unit_grads(number, size=CHUNK):
        grads = weight_grads(line.after(turned_ffn), acts[1:3], size, number)
        if size == CHUNK:
            line.push(grads[0], column("gate", number))
            line.push(grads[1], column("up", number))
        else:
            line.push(jnp.concatenate(grads, axis=1), column("gate", number, size), column("up", number, size))
        line.mark(grads[0])

    unit_grads(0)
    line.tick()
    number = 1
    while number < units // CHUNK:
        count = min(2, units // CHUNK - number)
        *acts, down = ffn(line.after(normed_ffn), grad_out, *weights, CHUNK, number, count, acts)
        for j in range(count):
            line.push(down[j * width : (j + 1) * width], stacked("down", number + j))
        line.mark(down)
        number += count
        line.tick()
    tail = []
    if rest:
        *acts, down = ffn(line.after(normed_ffn), grad_out, *weights, rest, units // rest - 1, 1, acts)
        tail.append(down)
        line.mark(down)
    hidden, grad_gate, grad_up = acts
    unit_grads(1)
    line.tick()
    part = (dot_nt(line.after(grad_gate), w_gate) + dot_nt(grad_up, w_up)).astype(BF16)
    part_other = exchange(part, "tensor")
    line.mark(part)
    line.tick()
    unit_grads(2)
    line.tick()
    grad_middle, grad_attn, grad_gain_ffn = norm_back(
        line.after(part), part_other, middle, gain_ffn, grad_out, True
    )
    line.mark(grad_attn)
    line.tick()

    grad_heads = dot_nt(line.after(grad_attn), w_out).astype(BF16)
    line.mark(grad_heads)
    line.tick()
    pairs = queries.shape[1] // (2 * HD)
    grads = [None] * 3
    for first in range(pairs):
        grads = attend_back(queries, keys, mixed, probs, line.after(grad_heads), cos, sin, first, 1, grads)
        line.mark(grads[0])
        if first == 0:
            for number in range(3, units // CHUNK):
                unit_grads(number)
            if rest:
                unit_grads(units // rest - 1, rest)
        line.tick()
    grad_query, grad_key, half_mixed = grads
    arrived = [send(half_mixed, (s, 0)) for s in range(1, n_sections)]
    for number in range(heads.shape[1] // CHUNK):
        line.push(stacked_grads(line.after(heads), grad_attn, number), stacked("out", number))
    line.mark(line.parts[-1])
    line.tick()

    def column_grads(name, grad):
        for number in range(grad.shape[1] // CHUNK):
            lo = number * CHUNK
            line.push(dot_tn(normed, line.after(grad)[:, lo : lo + CHUNK]).astype(BF16), column(name, number))
        line.mark(*line.parts[-2:])

    column_grads("query", grad_query)
    line.tick()
    column_grads("key", grad_key)
    line.tick()
    part = dot_nt(line.after(grad_query), w_query) + dot_nt(grad_key, w_key)
    line.mark(part)
    line.tick()
    part_result = dot(line.after(hidden), w_down).astype(BF16)
    result_other = exchange(part_result, "tensor")
    line.mark(part_result)
    line.tick()
    result = (middle + (line.after(part_result).astype(F32) + result_other.astype(F32))).astype(BF16)
    line.mark(result)
    line.tick()
    half_mixed = line.after(half_mixed).astype(F32)
    first_total = half_mixed
    for block in arrived:
        first_total = first_total + block.astype(F32)
    grad_value = (half_mixed + jnp.where(section == 0, first_total, 0.0)).astype(BF16)
    column_grads("value", grad_value)
    line.tick()
    part = (part + dot_nt(line.after(grad_value), w_value)).astype(BF16)
    part_other = exchange(part, "tensor")
    line.mark(part)
    line.tick()
    grad_input, grad_gain_attn = norm_back(line.after(part), part_other, x, gain_attn, grad_middle, False)
    line.mark(grad_input)
    gains = jnp.concatenate([grad_gain_attn, grad_gain_ffn], axis=0).reshape(-1, CHUNK).astype(BF16)
    tail_rows = sum(t.shape[0] for t in tail)
    tail.append(jnp.pad(gains, ((0, width - tail_rows - gains.shape[0]), (0, 0))))
    line.push(jnp.concatenate(tail, axis=0), column("tail", 0))
    line.finish()

    outs = line.outs
    tail = outs["tail"]
    gains = tail[tail_rows : tail_rows + gains.shape[0]].reshape(2, width)
    if rest:
        last = jnp.concatenate([tail[lo : lo + rest] for lo in range(0, tail_rows, rest)], axis=1)
        outs["down"] = lax.dynamic_update_slice(outs["down"], last, (units - rest, 0))
    return (
        result[None],
        grad_input[None],
        gains[0:1],
        *(outs[name][None] for name in ("query", "key", "value", "out")),
        gains[1:2],
        *(outs[name][None] for name in ("gate", "up", "down")),
    )


def solution(mesh):
    sizes = dict(mesh.shape)
    token = P("section", "dp", None)
    gain = P("section", None)
    wide, tall = P("section", None, "tensor"), P("section", "tensor", None)
    return jax.shard_map(
        lambda *args: shards(sizes, *args),
        mesh=mesh,
        in_specs=(token, P("dp", None), gain, wide, wide, wide, tall, gain, wide, wide, tall, token),
        out_specs=(token, token, gain, wide, wide, wide, tall, gain, wide, wide, tall),
        check_vma=False,
    )
```

```python
import jax
import jax.numpy as jnp
from jax import lax
from jax.experimental import pallas as pl
from jax.experimental.pallas import tpu as pltpu
from jax.sharding import PartitionSpec as P

HD = 64
WINDOW = 512
EPSILON = 1e-06
MASKED = -1e30
F32 = jnp.float32
BF16 = jnp.bfloat16
MIB = 1024 * 1024
UNITS = 384
CHUNK = 256


def dot(left, right):
    return lax.dot_general(left, right, (((1,), (0,)), ((), ())), preferred_element_type=F32)


def dot_nt(left, right):
    return lax.dot_general(left, right, (((1,), (1,)), ((), ())), preferred_element_type=F32)


def dot_tn(left, right):
    return lax.dot_general(left, right, (((0,), (0,)), ((), ())), preferred_element_type=F32)


def call(kernel, grid, ins, outs, args, vmem, scratch=(), into=None):
    into = {o: array for o, array in (into or {}).items() if array is not None}
    ins, args, n = list(ins), list(args), len(args)
    body = kernel
    if into:
        ins += [pl.BlockSpec(memory_space=pl.ANY)] * len(into)
        args += list(into.values())

        def body(*refs):
            kernel(*refs[:n], *refs[n + len(into) :])

    return pl.pallas_call(
        body,
        grid=grid,
        in_specs=ins,
        out_specs=[spec for spec, _, _ in outs],
        out_shape=[jax.ShapeDtypeStruct(shape, dtype) for _, shape, dtype in outs],
        scratch_shapes=list(scratch),
        input_output_aliases={n + j: o for j, o in enumerate(into)},
        compiler_params=pltpu.CompilerParams(vmem_limit_bytes=vmem * MIB),
        cost_estimate=pl.CostEstimate(flops=1, bytes_accessed=1, transcendentals=0),
    )(*args)


def rows(block, width):
    return pl.BlockSpec((block, width), lambda i: (i, 0))


def whole(*shape):
    return pl.BlockSpec(shape, lambda i: (0,) * len(shape))


def columns(height, block, first=0):
    return pl.BlockSpec((height, block), lambda i: (0, i + first))


def value_kernel(x_ref, gain_ref, w_ref, normed_ref, *value_refs):
    x = x_ref[...].astype(F32)
    inv_rms = lax.rsqrt(jnp.mean(x * x, axis=1, keepdims=True) + EPSILON)
    normed = (x * inv_rms * gain_ref[...]).astype(BF16)
    normed_ref[...] = normed
    values = dot(normed, w_ref[...]).astype(BF16)
    cut = values.shape[1] // len(value_refs)
    for j, ref in enumerate(value_refs):
        ref[...] = values[:, j * cut : (j + 1) * cut]


def value_proj(x, gain, w_value):
    tokens, width = x.shape
    half = w_value.shape[1] // 2
    block = 256
    return call(
        value_kernel,
        (tokens // block,),
        [rows(block, width), whole(1, width), whole(width, 2 * half)],
        [(rows(block, width), (tokens, width), BF16)] + [(rows(block, half), (tokens, half), BF16)] * 2,
        (x, gain, w_value),
        60,
    )


def swap_halves(u):
    lane = lax.broadcasted_iota(jnp.int32, u.shape, 1) % HD
    return jnp.where(lane < HD // 2, pltpu.roll(u, 128 - HD // 2, 1), pltpu.roll(u, HD // 2, 1))


def query_key_kernel(n_ref, wq_ref, wk_ref, cos_ref, sin_ref, q_ref, k_ref, turned_ref):
    normed = n_ref[...]
    cos, sin = cos_ref[...], sin_ref[...]
    for w_ref, o_ref in ((wq_ref, q_ref), (wk_ref, k_ref)):
        u = dot(normed, w_ref[...])
        for lo in range(0, u.shape[1], 128):
            part = u[:, lo : lo + 128]
            o_ref[:, lo : lo + 128] = (part * cos + swap_halves(part) * sin).astype(BF16)
    turned_ref[...] = normed.T


def query_key_proj(normed, w_query, w_key, cos, sin):
    tokens, width = normed.shape
    out = w_query.shape[1]
    block = 256
    return call(
        query_key_kernel,
        (tokens // block,),
        [rows(block, width), whole(width, out), whole(width, out), rows(block, 128), rows(block, 128)],
        [
            (rows(block, out), (tokens, out), BF16),
            (rows(block, out), (tokens, out), BF16),
            (columns(width, block), (width, tokens), BF16),
        ],
        (normed, w_query, w_key, cos, sin),
        32,
    )


def row_starts(len_ref, first, count):
    place = first + lax.broadcasted_iota(jnp.int32, (count, 1), 0)
    start = jnp.zeros((count, 1), jnp.int32)
    end = 0
    for j in range(len_ref.shape[1]):
        end = end + len_ref[0, j]
        start = jnp.where(place >= end, end, start)
    return place, start


def band(len_ref, first, count):
    low = max(0, first - WINDOW)
    place, start = row_starts(len_ref, first, count)
    col = low + lax.broadcasted_iota(jnp.int32, (count, first + count - low), 1)
    return low, (col >= start) & (col <= place)


def head_masks(count):
    lane = lax.broadcasted_iota(jnp.int32, (count, 2 * HD), 1)
    return lane < HD, lane >= HD


def probs_kernel(len_ref, q_ref, k_ref, probs_ref):
    tokens = q_ref.shape[0]
    block = 256
    for at in range(0, tokens, block):
        low, allowed = band(len_ref, at, block)
        queries = q_ref[at : at + block, :] * BF16(HD**-0.5)
        keys = k_ref[low : at + block, :]
        for h, mask in enumerate(head_masks(block)):
            scores = dot_nt(jnp.where(mask, queries, BF16(0)), keys)
            scores = jnp.where(allowed, scores, MASKED)
            exps = jnp.exp(scores - jnp.max(scores, axis=1, keepdims=True))
            total = jnp.sum(exps, axis=1, keepdims=True)
            probs_ref[h, at : at + block, : at + block - low] = (exps * (1.0 / total)).astype(BF16)


def band_width(tokens):
    return min(tokens, WINDOW + 256)


def probabilities(lengths, queries, keys):
    tokens, width = queries.shape
    pair = columns(tokens, 2 * HD)
    wide = band_width(tokens)
    return call(
        probs_kernel,
        (width // (2 * HD),),
        [pl.BlockSpec(memory_space=pltpu.SMEM), pair, pair],
        [(pl.BlockSpec((2, tokens, wide), lambda i: (i, 0, 0)), (width // HD, tokens, wide), BF16)],
        (lengths, queries, keys),
        40,
    )[0]


def heads_kernel(n_arrived, places, section_ref, *refs):
    probs_ref, own_refs, arrived = refs[0], refs[1:3], refs[3 : 3 + n_arrived]
    w_ref, heads_ref, mixed_ref, part_ref = refs[3 + n_arrived :]
    block = heads_ref.shape[0]
    half = own_refs[0].shape[1]
    step = pl.program_id(0)

    for section, sources in enumerate(places):

        @pl.when((step == 0) & (section_ref[0] == section))
        def _():
            for j, source in enumerate(sources):
                first_ref = own_refs[j] if source is None else arrived[source]
                mixed_ref[:, j * half : (j + 1) * half] = (
                    0.5 * own_refs[j][...].astype(F32) + 0.5 * first_ref[...].astype(F32)
                ).astype(BF16)

    first_mask, _ = head_masks(block)
    for i in range(own_refs[0].shape[0] // block):
        at = i * block
        low = max(0, at - WINDOW)

        @pl.when(step == i)
        def _():
            for pair in range(heads_ref.shape[1] // (2 * HD)):
                lanes = slice(pair * 2 * HD, (pair + 1) * 2 * HD)
                values = mixed_ref[low : at + block, lanes]
                both = [dot(probs_ref[2 * pair + h, :, : at + block - low], values) for h in range(2)]
                heads_ref[:, lanes] = jnp.where(first_mask, both[0], both[1]).astype(BF16)

    part_ref[...] = dot(heads_ref[...], w_ref[...]).astype(BF16)


def heads_proj(section, probs, own, arrived, places, w_out):
    tokens, half = own[0].shape
    width, model = w_out.shape
    n_heads, _, wide = probs.shape
    block = 256
    return call(
        lambda *refs: heads_kernel(len(arrived), places, *refs),
        (tokens // block,),
        [pl.BlockSpec(memory_space=pltpu.SMEM), pl.BlockSpec((n_heads, block, wide), lambda i: (0, i, 0))]
        + [whole(tokens, half)] * (2 + len(arrived))
        + [whole(width, model)],
        [
            (rows(block, width), (tokens, width), BF16),
            (whole(tokens, width), (tokens, width), BF16),
            (rows(block, model), (tokens, model), BF16),
        ],
        (section.astype(jnp.int32)[None], probs, *own, *arrived, w_out),
        40,
    )


def attend_back_kernel(
    q_ref, k_ref, mixed_ref, probs_ref, attn_ref, w_ref, cos_ref, sin_ref, dq_ref, dk_ref, half_ref, grad_ref, key_acc, value_acc
):
    tokens = q_ref.shape[0]
    block = 256
    key_acc[...] = jnp.zeros_like(key_acc)
    value_acc[...] = jnp.zeros_like(value_acc)
    grad_ref[...] = dot_nt(attn_ref[...], w_ref[...]).astype(BF16)

    def turned_back(grads, at, count):
        cos, sin = cos_ref[at : at + count, :], sin_ref[at : at + count, :]
        return (grads * cos - swap_halves(grads) * sin).astype(BF16)

    masks = head_masks(block)
    for at in range(0, tokens, block):
        low = max(0, at - WINDOW)
        grads = grad_ref[at : at + block, :]
        queries_turned = (q_ref[at : at + block, :] * BF16(HD**-0.5)).T
        grads_turned = grads.T
        keys = k_ref[low : at + block, :]
        values = mixed_ref[low : at + block, :]
        parts = []
        for h, mask in enumerate(masks):
            lanes = slice(h * HD, (h + 1) * HD)
            probs_low = probs_ref[h, at : at + block, : at + block - low]
            probs = probs_low.astype(F32)
            grad_probs = dot_nt(jnp.where(mask, grads, BF16(0)), values)
            inner = jnp.sum(probs * grad_probs, axis=1, keepdims=True)
            grad_scores = (probs * (grad_probs - inner)).astype(BF16)
            parts.append(dot(grad_scores, keys))
            key_acc[lanes, low : at + block] += dot(queries_turned[lanes], grad_scores)
            value_acc[lanes, low : at + block] += dot(grads_turned[lanes], probs_low)
        grad_query = jnp.where(masks[0], parts[0], parts[1]) * HD**-0.5
        dq_ref[at : at + block, :] = turned_back(grad_query, at, block)
    for at in range(0, tokens, block):
        dk_ref[at : at + block, :] = turned_back(key_acc[:, at : at + block].T, at, block)
        half_ref[at : at + block, :] = (0.5 * value_acc[:, at : at + block].T).astype(BF16)


def attend_back(queries, keys, mixed, probs, grad_attn, w_out, cos, sin, first, count, into):
    tokens, width = queries.shape
    model = w_out.shape[1]
    pair = columns(tokens, 2 * HD, first)
    wide = probs.shape[2]
    return call(
        attend_back_kernel,
        (count,),
        [pair, pair, pair, pl.BlockSpec((2, tokens, wide), lambda i: (i + first, 0, 0)), whole(tokens, model)]
        + [pl.BlockSpec((2 * HD, model), lambda i: (i + first, 0)), whole(tokens, 128), whole(tokens, 128)],
        [(pair, (tokens, width), BF16)] * 3,
        (queries, keys, mixed, probs, grad_attn, w_out, cos, sin),
        26,
        scratch=[pltpu.VMEM((tokens, 2 * HD), BF16)] + [pltpu.VMEM((2 * HD, tokens), F32)] * 2,
        into=dict(enumerate(into)),
    )


def unit_acts(normed, grad_out, w_gate, w_up, w_down, hidden_ref, dg_ref, du_ref):
    gate = dot(normed, w_gate)
    up = dot(normed, w_up)
    grad_hidden = dot_nt(grad_out, w_down)
    sig = jax.nn.sigmoid(gate)
    silu = gate * sig
    hidden = (silu * up).astype(BF16)
    hidden_ref[...] = hidden
    dg_ref[...] = (grad_hidden * up * (sig * (1.0 + gate * (1.0 - sig)))).astype(BF16)
    du_ref[...] = (grad_hidden * silu).astype(BF16)
    return hidden


def entry_kernel(n, x_ref, own_ref, other_ref, gain_ref, grad_ref, *refs):
    gates, ups, downs = (refs[j * n : (j + 1) * n] for j in range(3))
    normed_ref, hidden_ref, dg_ref, du_ref, gwd_ref, acc = refs[3 * n :]
    step = pl.program_id(0)
    middle = x_ref[...].astype(F32) + (own_ref[...].astype(F32) + other_ref[...].astype(F32))
    inv_rms = lax.rsqrt(jnp.mean(middle * middle, axis=1, keepdims=True) + EPSILON)
    normed = (middle * inv_rms * gain_ref[...]).astype(BF16)
    normed_ref[...] = normed
    w_gate, w_up = (jnp.concatenate([r[...] for r in group], axis=1) for group in (gates, ups))
    w_down = jnp.concatenate([r[...] for r in downs], axis=0)
    grad_out = grad_ref[...]
    hidden = unit_acts(normed, grad_out, w_gate, w_up, w_down, hidden_ref, dg_ref, du_ref)
    term = dot(hidden.T, grad_out)
    last = pl.num_programs(0) - 1

    @pl.when(step == 0)
    def _():
        acc[...] = term

    @pl.when((step > 0) & (step < last))
    def _():
        acc[...] += term

    @pl.when(step == last)
    def _():
        gwd_ref[...] = (acc[...] + term).astype(BF16)


def entry(x, own, other, gain, grad_out, w_gate, w_up, w_down, units):
    tokens, width = x.shape
    block = 512
    n = units // 128
    at = w_gate.shape[1] // 128 - n

    def wide(j):
        return pl.BlockSpec((width, 128), lambda i: (0, at + j))

    def tall(j):
        return pl.BlockSpec((128, width), lambda i: (at + j, 0))

    return call(
        lambda *refs: entry_kernel(n, *refs),
        (tokens // block,),
        [rows(block, width)] * 3
        + [whole(1, width), rows(block, width)]
        + [wide(j) for j in range(n)] * 2
        + [tall(j) for j in range(n)],
        [(rows(block, width), (tokens, width), BF16)]
        + [(rows(block, units), (tokens, units), BF16)] * 3
        + [(whole(units, width), (units, width), BF16)],
        (x, own, other, gain, grad_out, *[w_gate] * n, *[w_up] * n, *[w_down] * n),
        60,
        scratch=[pltpu.VMEM((units, width), F32)],
    )


def ffn_kernel(normed_ref, grad_ref, wg_ref, wu_ref, wd_ref, hidden_ref, dg_ref, du_ref, gwd_ref):
    grad_out = grad_ref[...]
    hidden = unit_acts(normed_ref[...], grad_out, wg_ref[...], wu_ref[...], wd_ref[...], hidden_ref, dg_ref, du_ref)
    gwd_ref[...] = dot(hidden.T, grad_out).astype(BF16)


def ffn(normed, grad_out, w_gate, w_up, w_down, units, number, count, into):
    tokens, width = normed.shape
    return call(
        ffn_kernel,
        (1,),
        [whole(tokens, width)] * 2
        + [columns(width, units, number)] * 2
        + [pl.BlockSpec((units, width), lambda i: (number, 0))],
        [(columns(tokens, units, number), (tokens, units * count), BF16)] * 3
        + [(whole(units, width), (units, width), BF16)],
        (normed, grad_out, w_gate, w_up, w_down),
        40,
        into=dict(enumerate(into)),
    )


def turn_kernel(ref, out_ref):
    out_ref[...] = ref[...].T


def turned(array):
    tall, wide = array.shape
    block = 256
    return call(
        turn_kernel, (tall // block,), [rows(block, wide)], [(columns(wide, block), (wide, tall), array.dtype)], (array,), 24
    )[0]


def weight_grads_kernel(turned_ref, *refs):
    half = len(refs) // 2
    for d_ref, o_ref in zip(refs[:half], refs[half:]):
        o_ref[...] = dot(turned_ref[...], d_ref[...]).astype(BF16)


def weight_grads(left, grads, units, numbers):
    width, tokens = left.shape
    block = 512
    return call(
        weight_grads_kernel,
        (width // block,),
        [rows(block, tokens)] + [pl.BlockSpec((tokens, units), lambda i, at=at: (0, at)) for at in numbers],
        [(rows(block, units), (width, units), BF16)] * len(grads),
        (left, *grads),
        20,
    )


def row_grads_kernel(left_ref, right_ref, out_ref, left):
    @pl.when(pl.program_id(0) == 0)
    def _():
        left[...] = left_ref[...].T

    out_ref[...] = dot(left[...], right_ref[...]).astype(BF16)


def row_grads(left, right, number):
    tokens, width = right.shape
    block = 512
    return call(
        row_grads_kernel,
        (width // block,),
        [pl.BlockSpec((tokens, CHUNK), lambda i: (0, number)), columns(tokens, block)],
        [(columns(CHUNK, block), (CHUNK, width), BF16)],
        (left, right),
        24,
        scratch=[pltpu.VMEM((CHUNK, tokens), BF16)],
    )[0]


def products_kernel(turn, counts, *refs):
    out_ref = refs[-1]
    n = sum(counts)
    lefts, weights = list(refs[:n]), refs[n:-1]
    total = None
    for count, w_ref in zip(counts, weights):
        at = 0
        for _ in range(count):
            left = lefts.pop(0)
            deep = left.shape[1]
            if turn:
                term = dot_nt(left[...], w_ref[:, at : at + deep])
            else:
                term = dot(left[...], w_ref[at : at + deep, :])
            at += deep
            total = term if total is None else total + term
    out_ref[...] = total.astype(BF16)


def products(pairs, turn):
    counts = [len(lefts) for lefts, _ in pairs]
    lefts = [left for group, _ in pairs for left in group]
    weights = [w for _, w in pairs]
    tokens = lefts[0].shape[0]
    width = weights[0].shape[0 if turn else 1]
    block = 256
    specs = [rows(block, w.shape[1]) if turn else columns(w.shape[0], block) for w in weights]
    return call(
        lambda *refs: products_kernel(turn, counts, *refs),
        (width // block,),
        [whole(*left.shape) for left in lefts] + specs,
        [(columns(tokens, block), (tokens, width), BF16)],
        (*lefts, *weights),
        26,
    )[0]


def summed(refs):
    total = refs[0][...].astype(F32)
    if len(refs) > 1:
        total = total + (refs[1][...].astype(F32) + refs[2][...].astype(F32))
    return total


def norm_back_kernel(n, low, dn_ref, do_ref, gain_ref, base_ref, *refs):
    values = summed(refs[:n])
    out_ref, more, gain_grad_ref = refs[n], refs[n + 1 : -1], refs[-1]
    grad_normed = dn_ref[...].astype(F32) + do_ref[...].astype(F32)
    inv_rms = lax.rsqrt(jnp.mean(values * values, axis=1, keepdims=True) + EPSILON)
    weighted = grad_normed * gain_ref[...]
    inner = jnp.mean(weighted * values, axis=1, keepdims=True)
    out = base_ref[...].astype(F32) + inv_rms * weighted - values * (inv_rms * inv_rms * inv_rms) * inner
    out_ref[...] = out
    if low:
        more[0][...] = out.astype(BF16)

    @pl.when(pl.program_id(0) == 0)
    def _():
        gain_grad_ref[...] = jnp.zeros_like(gain_grad_ref)

    gain_grad_ref[...] += jnp.sum(grad_normed * values * inv_rms, axis=0, keepdims=True)


def norm_back(own, other, values, gain, base, low):
    tokens, width = own.shape
    block = 256
    outs = [(rows(block, width), (tokens, width), F32)]
    if low:
        outs.append((rows(block, width), (tokens, width), BF16))
    outs.append((whole(1, width), (1, width), F32))
    return call(
        lambda *refs: norm_back_kernel(len(values), low, *refs),
        (tokens // block,),
        [rows(block, width)] * 2 + [whole(1, width)] + [rows(block, width)] * (1 + len(values)),
        outs,
        (own, other, gain, base, *values),
        28,
    )


def result_kernel(own_ref, other_ref, *refs):
    refs[-1][...] = (summed(refs[:-1]) + (own_ref[...].astype(F32) + other_ref[...].astype(F32))).astype(BF16)


def block_result(own, other, values):
    tokens, width = own.shape
    block = 256
    return call(
        result_kernel,
        (tokens // block,),
        [rows(block, width)] * (2 + len(values)),
        [(rows(block, width), (tokens, width), BF16)],
        (own, other, *values),
        24,
    )[0]


def relay_kernel(section_ref, half_ref, left_ref, right_ref, out_ref):
    cut = left_ref.shape[1]
    out_ref[...] = half_ref[...]
    for section, ref, lanes in ((1, left_ref, slice(0, cut)), (2, right_ref, slice(cut, 2 * cut))):

        @pl.when(section_ref[0] == section)
        def _():
            out_ref[:, lanes] = (half_ref[:, lanes].astype(F32) + ref[...].astype(F32)).astype(BF16)


def relayed(section, half, left, right):
    tokens, width = half.shape
    block = 512
    return call(
        relay_kernel,
        (tokens // block,),
        [pl.BlockSpec(memory_space=pltpu.SMEM), rows(block, width)] + [rows(block, width // 2)] * 2,
        [(rows(block, width), (tokens, width), BF16)],
        (section.astype(jnp.int32)[None], half, left, right),
        16,
    )[0]


def first_grad_kernel(section_ref, half_ref, *refs):
    out_ref = refs[-1]

    @pl.when(section_ref[0] == 0)
    def _():
        half = half_ref[...].astype(F32)
        total = half
        for ref in refs[:-1]:
            total = total + ref[...].astype(F32)
        out_ref[...] = (half + total).astype(BF16)

    @pl.when(section_ref[0] != 0)
    def _():
        out_ref[...] = half_ref[...]


def first_grad(section, half, arrived):
    tokens, width = half.shape
    block = 256
    return call(
        first_grad_kernel,
        (tokens // block,),
        [pl.BlockSpec(memory_space=pltpu.SMEM)] + [rows(block, width)] * (1 + len(arrived)),
        [(rows(block, width), (tokens, width), BF16)],
        (section.astype(jnp.int32)[None], half, *arrived),
        24,
    )[0]


def tie(*values):
    return lax.optimization_barrier(values)


def chosen_call(kernel, grid, flags, ins, out, shape, dtype, args, into=None):
    def spec(block, flag):
        return pl.BlockSpec(block, lambda i, j, flags: (i * flags[flag], j * flags[flag]))

    block, at = out
    held = [] if into is None else [into]
    n = len(args)

    def body(flags_ref, *refs):
        kernel(flags_ref, *refs[:n], *refs[n + len(held) :])

    return pl.pallas_call(
        body,
        grid_spec=pltpu.PrefetchScalarGridSpec(
            num_scalar_prefetch=1,
            grid=grid,
            in_specs=[spec(*one) for one in ins] + [pl.BlockSpec(memory_space=pl.ANY)] * len(held),
            out_specs=pl.BlockSpec(block, lambda i, j, flags: at(i, j)),
        ),
        out_shape=jax.ShapeDtypeStruct(shape, dtype),
        input_output_aliases={1 + n: 0} if held else {},
        compiler_params=pltpu.CompilerParams(vmem_limit_bytes=10 * MIB),
        cost_estimate=pl.CostEstimate(flops=1, bytes_accessed=1, transcendentals=0),
    )(flags, *args, *held)


MID, END = 0, 1


def add_kernel(flags_ref, one_ref, two_ref, out_ref):
    @pl.when(flags_ref[MID] == 1)
    def _():
        out_ref[...] = (one_ref[...].astype(F32) + two_ref[...].astype(F32)).astype(BF16)


def put_kernel(flags_ref, mid_ref, end_ref, out_ref):
    @pl.when(flags_ref[MID] == 1)
    def _():
        out_ref[...] = mid_ref[...].astype(F32)

    @pl.when(flags_ref[END] == 1)
    def _():
        out_ref[...] = end_ref[...].astype(F32)


class Line:
    def __init__(self, axis, size, shapes, depth=3):
        self.axis, self.size, self.shapes, self.depth = axis, size, shapes, depth
        place = lax.axis_index(axis)
        end = (place == 0) | (place == 3)
        self.flags = jnp.stack([jnp.logical_not(end), end]).astype(jnp.int32)
        self.parts, self.places = [], []
        self.inward, self.across, self.outward, self.half, self.total = {}, {}, {}, {}, {}
        self.outs = {name: None for name in shapes}
        self.at = self.started = 0
        self.clock = []

    def after(self, *values):
        if not self.clock:
            return values if len(values) > 1 else values[0]
        held = tie(*values, *self.clock)[: len(values)]
        return held if len(values) > 1 else held[0]

    def mark(self, *values):
        self.clock = list(values)

    def push(self, part, *place):
        self.parts.append(part)
        self.places.append(place)
        self.start()

    def start(self):
        while self.size == 4 and self.started < len(self.parts) and self.started < self.at + self.depth:
            i = self.started
            self.parts[i] = self.after(self.parts[i])
            self.inward[i] = lax.ppermute(self.parts[i], self.axis, [(0, 1), (3, 2)])
            self.started += 1

    def add(self, one, two):
        tall, wide = one.shape
        block = (min(tall, 512), wide)
        ins = [(block, MID)] * 2
        return chosen_call(
            add_kernel, (tall // block[0], 1), self.flags, ins, (block, lambda i, j: (i, j)), one.shape, BF16, (one, two)
        )

    def step(self, drain=False):
        i, n = self.at, len(self.parts)
        if self.size != 4 or i >= n and not drain:
            return
        self.at += 1
        if i < n:
            part, arrived = self.after(self.parts[i], self.inward[i])
            self.half[i] = self.add(part, arrived)
            self.across[i] = lax.ppermute(self.half[i], self.axis, [(1, 2), (2, 1)])
            self.mark(self.half[i])
        if 0 <= i - 1 < n:
            half, arrived = self.after(self.half[i - 1], self.across[i - 1])
            self.total[i - 1] = self.add(half, arrived)
            self.outward[i - 1] = lax.ppermute(self.total[i - 1], self.axis, [(1, 0), (2, 3)])
            self.mark(self.total[i - 1])
        self.start()
        if 0 <= i - 2 < n:
            total, arrived = self.after(self.total[i - 2], self.outward[i - 2])
            name, block, at = self.places[i - 2]
            grid = tuple(s // b for s, b in zip(total.shape, block))
            self.outs[name] = chosen_call(
                put_kernel,
                grid,
                self.flags,
                [(block, MID), (block, END)],
                (block, at),
                self.shapes[name],
                F32,
                (total, arrived),
                self.outs[name],
            )
            self.mark(self.outs[name])

    def finish(self):
        if self.size == 4:
            while self.at < len(self.parts) + 2:
                self.step(True)
            return
        for part, (name, block, at) in zip(self.parts, self.places):
            if self.outs[name] is None:
                self.outs[name] = jnp.zeros(self.shapes[name], F32)
            where = tuple(b * o for b, o in zip(block, at(0, 0)))
            self.outs[name] = lax.dynamic_update_slice(self.outs[name], lax.psum(part, self.axis).astype(F32), where)


def tables(lengths_row, tokens):
    seqs = lengths_row.shape[0]
    slot = jnp.arange(seqs, dtype=jnp.int32)
    ends = jnp.sum(jnp.where(slot[None, :] <= slot[:, None], lengths_row[None, :], 0), axis=1)
    places = jnp.arange(tokens, dtype=jnp.int32)
    start = jnp.sum(jnp.where(places[:, None] >= ends[None, :], lengths_row[None, :], 0), axis=1)
    position = (places - start).astype(F32)
    inv_freq = 10000.0 ** (-(jnp.arange(HD // 2, dtype=F32) * 2.0 / HD))
    angles = position[:, None] * inv_freq[None, :]
    cos, sin = jnp.cos(angles), jnp.sin(angles)
    return jnp.concatenate([cos] * 4, axis=1), jnp.concatenate([-sin, sin, -sin, sin], axis=1)


def exchange(part, axis):
    return lax.ppermute(part, axis, [(0, 1), (1, 0)])


def shards(sizes, *args):
    (x, lengths, gain_attn, w_query, w_key, w_value, w_out, gain_ffn, w_gate, w_up, w_down, grad_out) = args
    x, w_query, w_key, w_value, w_out, w_gate, w_up, w_down, grad_out = (
        a[0] for a in (x, w_query, w_key, w_value, w_out, w_gate, w_up, w_down, grad_out)
    )
    tokens, width = x.shape
    units = w_gate.shape[1]
    n_blocks = (units - 1) // UNITS
    rest = units - n_blocks * UNITS
    n_sections = sizes["section"]
    section = lax.axis_index("section")
    outputs = {"query": w_query, "key": w_key, "value": w_value, "out": w_out, "gate": w_gate, "up": w_up, "down": w_down}
    shapes = {name: w.shape for name, w in outputs.items()}
    shapes["gains"] = (16, width)
    line = Line("dp", sizes["dp"], shapes)

    def put_columns(name, first, wide):
        return name, (512, wide), lambda i, j: (i, first + j)

    def put_rows(name, first, tall):
        return name, (tall, width), lambda i, j: (first + i, 0)

    normed, *own = value_proj(x, gain_attn, w_value)

    def send(block, *pairs):
        return lax.ppermute(block, "section", list(pairs))

    relay = n_sections == 4
    if relay:
        one, two = send(own[0], (0, 1)), send(own[1], (0, 2))
    cos, sin = tables(lengths[0], tokens)
    queries, keys, turned_attn = query_key_proj(normed, w_query, w_key, cos, sin)
    if relay:
        one, two, queries = tie(one, two, queries)
        three = send(jnp.where(section == 0, own[1], one), (0, 1), (1, 3))
        four = send(jnp.where(section == 0, own[0], two), (0, 2), (2, 3))
        arrived = [one, two, three, four]
        places = [(None, None), (0, 2), (3, 1), (2, 3)]
    else:
        arrived = [send(half, (0, s)) for s in range(1, n_sections) for half in own]
        places = [(None, None)] + [(2 * s, 2 * s + 1) for s in range(n_sections - 1)]
    probs = probabilities(lengths, queries, keys)
    probs, *arrived = tie(probs, *arrived)
    heads, mixed, part = heads_proj(section, probs, own, arrived, places, w_out)
    middle = (x, part, exchange(part, "tensor"))

    weights = (w_gate, w_up, w_down)
    normed_ffn, *rest_acts, down = entry(*middle, gain_ffn, grad_out, *weights, rest)
    line.push(down, *put_rows("down", n_blocks * UNITS // 128, 128))
    line.mark(normed_ffn)
    turned_ffn = turned(line.after(normed_ffn))
    gate, up = weight_grads(turned_ffn, rest_acts[1:], rest, (0, 0))
    line.mark(gate, up)
    line.push(gate, *put_columns("gate", n_blocks * UNITS // 128, 128))
    line.push(up, *put_columns("up", n_blocks * UNITS // 128, 128))
    acts = [None] * 3
    for number in range(n_blocks):
        *acts, down = ffn(line.after(normed_ffn), grad_out, *weights, UNITS, number, n_blocks, acts)
        line.mark(down)
        line.push(down, *put_rows("down", number * UNITS // 128, 128))
        line.step()

    def unit_grads(number):
        if number < n_blocks:
            gate, up = weight_grads(line.after(turned_ffn), acts[1:], UNITS, (number, number))
            line.mark(gate, up)
            line.push(gate, *put_columns("gate", number, UNITS))
            line.push(up, *put_columns("up", number, UNITS))

    unit_grads(0)
    line.step()
    part = products([((acts[1], line.after(rest_acts[1])), w_gate), ((acts[2], rest_acts[2]), w_up)], True)
    part_other = exchange(part, "tensor")
    line.mark(part)
    line.step()
    unit_grads(1)
    line.step()
    grad_middle, grad_attn, grad_gain_ffn = norm_back(line.after(part), part_other, middle, gain_ffn, grad_out, True)
    line.mark(grad_attn)
    line.step()
    for number in range(2, n_blocks):
        unit_grads(number)
    for number in range(heads.shape[1] // CHUNK):
        part = row_grads(line.after(heads), grad_attn, number)
        line.mark(part)
        line.push(part, *put_rows("out", number * CHUNK // 128, 128))
    line.step()

    def column_grads(name, grad):
        numbers = tuple(range(grad.shape[1] // CHUNK))
        parts = weight_grads(line.after(turned_attn), [grad] * len(numbers), CHUNK, numbers)
        line.mark(*parts)
        for number, part in zip(numbers, parts):
            line.push(part, *put_columns(name, number, CHUNK))

    pairs = queries.shape[1] // (2 * HD)
    grads = [None] * 3
    for first in range(pairs):
        grads = attend_back(queries, keys, mixed, probs, line.after(grad_attn), w_out, cos, sin, first, 1, grads)
        line.mark(*grads)
        if first < pairs - 1:
            line.step()
    grad_query, grad_key, half_mixed = grads
    if relay:
        from_left, from_right = send(half_mixed[:, : half_mixed.shape[1] // 2], (3, 1)), send(
            half_mixed[:, half_mixed.shape[1] // 2 :], (3, 2)
        )
    else:
        arrived = [send(half_mixed, (s, 0)) for s in range(1, n_sections)]
    column_grads("query", grad_query)
    column_grads("key", grad_key)
    line.step()
    part_result = products([((acts[0], line.after(rest_acts[0])), w_down)], False)
    result_other = exchange(part_result, "tensor")
    line.mark(part_result)
    line.step()
    if relay:
        both = relayed(section, line.after(half_mixed), from_left, from_right)
        arrived = [send(both, (s, 0)) for s in (1, 2)]
        line.mark(both)
    line.step()
    result = block_result(line.after(part_result), result_other, middle)
    line.mark(result)
    line.step()
    grad_value = first_grad(section, line.after(half_mixed), arrived)
    column_grads("value", grad_value)
    part = products(
        [((line.after(grad_query),), w_query), ((grad_key,), w_key), ((grad_value,), w_value)], True
    )
    part_other = exchange(part, "tensor")
    line.mark(part)
    line.step()
    line.step()
    grad_input, grad_gain_attn = norm_back(line.after(part), part_other, (x,), gain_attn, grad_middle, False)
    line.mark(grad_input)
    gains = jnp.concatenate([grad_gain_attn, grad_gain_ffn], axis=0)
    gains = jnp.pad(gains, ((0, 14), (0, 0))).astype(BF16)
    line.push(gains, "gains", (16, width), lambda i, j: (0, 0))
    line.finish()

    outs = line.outs
    return (
        result[None],
        grad_input[None],
        outs["gains"][0:1],
        *(outs[name][None] for name in ("query", "key", "value", "out")),
        outs["gains"][1:2],
        *(outs[name][None] for name in ("gate", "up", "down")),
    )


def solution(mesh):
    sizes = dict(mesh.shape)
    token = P("section", "dp", None)
    gain = P("section", None)
    wide, tall = P("section", None, "tensor"), P("section", "tensor", None)
    return jax.shard_map(
        lambda *args: shards(sizes, *args),
        mesh=mesh,
        in_specs=(token, P("dp", None), gain, wide, wide, wide, tall, gain, wide, wide, tall, token),
        out_specs=(token, token, gain, wide, wide, wide, tall, gain, wide, wide, tall),
        check_vma=False,
    )
```

```python
import jax
import jax.numpy as jnp
from jax import lax
from jax.experimental import pallas as pl
from jax.experimental.pallas import tpu as pltpu
from jax.sharding import PartitionSpec as P

HD = 64
WINDOW = 512
EPSILON = 1e-06
MASKED = -1e30
F32 = jnp.float32
BF16 = jnp.bfloat16
MIB = 1024 * 1024
UNITS = 384
GWAIT = 4
LAST = 2
DEPTH = 3


def dot(left, right):
    return lax.dot_general(left, right, (((1,), (0,)), ((), ())), preferred_element_type=F32)


def dot_nt(left, right):
    return lax.dot_general(left, right, (((1,), (1,)), ((), ())), preferred_element_type=F32)


def dot_tn(left, right):
    return lax.dot_general(left, right, (((0,), (0,)), ((), ())), preferred_element_type=F32)


def call(kernel, grid, ins, outs, args, vmem, scratch=(), into=None, name=None):
    into = {o: array for o, array in (into or {}).items() if array is not None}
    ins, args, n = list(ins), list(args), len(args)
    body = kernel
    if into:
        ins += [pl.BlockSpec(memory_space=pl.ANY)] * len(into)
        args += list(into.values())

        def body(*refs):
            kernel(*refs[:n], *refs[n + len(into) :])

    return pl.pallas_call(
        body,
        grid=grid,
        name=name or kernel.__name__.removesuffix("_kernel"),
        in_specs=ins,
        out_specs=[spec for spec, _, _ in outs],
        out_shape=[jax.ShapeDtypeStruct(shape, dtype) for _, shape, dtype in outs],
        scratch_shapes=list(scratch),
        input_output_aliases={n + j: o for j, o in enumerate(into)},
        compiler_params=pltpu.CompilerParams(vmem_limit_bytes=vmem * MIB),
        cost_estimate=pl.CostEstimate(flops=1, bytes_accessed=1, transcendentals=0),
    )(*args)


def rows(block, width):
    return pl.BlockSpec((block, width), lambda i: (i, 0))


def whole(*shape):
    return pl.BlockSpec(shape, lambda i: (0,) * len(shape))


def held(*shape):
    return pl.BlockSpec(shape, lambda i: (0,) * len(shape), pipeline_mode=pl.Buffered(1))


def columns(height, block, first=0):
    return pl.BlockSpec((height, block), lambda i: (0, i + first))


def value_kernel(x_ref, gain_ref, w_ref, normed_ref, *value_refs):
    x = x_ref[...].astype(F32)
    inv_rms = lax.rsqrt(jnp.mean(x * x, axis=1, keepdims=True) + EPSILON)
    normed = (x * inv_rms * gain_ref[...]).astype(BF16)
    normed_ref[...] = normed
    values = dot(normed, w_ref[...]).astype(BF16)
    cut = values.shape[1] // len(value_refs)
    for j, ref in enumerate(value_refs):
        ref[...] = values[:, j * cut : (j + 1) * cut]


def value_proj(x, gain, w_value):
    tokens, width = x.shape
    half = w_value.shape[1] // 2
    block = 256
    return call(
        value_kernel,
        (tokens // block,),
        [rows(block, width), held(1, width), held(width, 2 * half)],
        [(rows(block, width), (tokens, width), BF16)] + [(rows(block, half), (tokens, half), BF16)] * 2,
        (x, gain, w_value),
        60,
    )


def swap_halves(u):
    lane = lax.broadcasted_iota(jnp.int32, u.shape, 1) % HD
    return jnp.where(lane < HD // 2, pltpu.roll(u, 128 - HD // 2, 1), pltpu.roll(u, HD // 2, 1))


def query_key_kernel(n_ref, wq_ref, wk_ref, cos_ref, sin_ref, q_ref, k_ref, turned_ref):
    normed = n_ref[...]
    cos, sin = cos_ref[...], sin_ref[...]
    for w_ref, o_ref in ((wq_ref, q_ref), (wk_ref, k_ref)):
        u = dot(normed, w_ref[...])
        for lo in range(0, u.shape[1], 128):
            part = u[:, lo : lo + 128]
            o_ref[:, lo : lo + 128] = (part * cos + swap_halves(part) * sin).astype(BF16)
    turned_ref[...] = normed.T


def query_key_proj(normed, w_query, w_key, cos, sin):
    tokens, width = normed.shape
    out = w_query.shape[1]
    block = 256
    return call(
        query_key_kernel,
        (tokens // block,),
        [rows(block, width), held(width, out), held(width, out), rows(block, 128), rows(block, 128)],
        [
            (rows(block, out), (tokens, out), BF16),
            (rows(block, out), (tokens, out), BF16),
            (columns(width, block), (width, tokens), BF16),
        ],
        (normed, w_query, w_key, cos, sin),
        32,
    )


def row_starts(len_ref, first, count):
    place = first + lax.broadcasted_iota(jnp.int32, (count, 1), 0)
    start = jnp.zeros((count, 1), jnp.int32)
    end = 0
    for j in range(len_ref.shape[1]):
        end = end + len_ref[0, j]
        start = jnp.where(place >= end, end, start)
    return place, start


def band(len_ref, first, count):
    low = max(0, first - WINDOW)
    place, start = row_starts(len_ref, first, count)
    col = low + lax.broadcasted_iota(jnp.int32, (count, first + count - low), 1)
    return low, (col >= start) & (col <= place)


def head_masks(count):
    lane = lax.broadcasted_iota(jnp.int32, (count, 2 * HD), 1)
    return lane < HD, lane >= HD


def probs_kernel(len_ref, q_ref, k_ref, probs_ref):
    tokens = q_ref.shape[0]
    block = 256
    for at in range(0, tokens, block):
        low, allowed = band(len_ref, at, block)
        queries = q_ref[at : at + block, :] * BF16(HD**-0.5)
        keys = k_ref[low : at + block, :]
        for h, mask in enumerate(head_masks(block)):
            scores = dot_nt(jnp.where(mask, queries, BF16(0)), keys)
            scores = jnp.where(allowed, scores, MASKED)
            exps = jnp.exp(scores - jnp.max(scores, axis=1, keepdims=True))
            total = jnp.sum(exps, axis=1, keepdims=True)
            probs_ref[h, at : at + block, : at + block - low] = (exps * (1.0 / total)).astype(BF16)


def band_width(tokens):
    return min(tokens, WINDOW + 256)


def probabilities(lengths, queries, keys):
    tokens, width = queries.shape
    pair = columns(tokens, 2 * HD)
    wide = band_width(tokens)
    return call(
        probs_kernel,
        (width // (2 * HD),),
        [pl.BlockSpec(memory_space=pltpu.SMEM), pair, pair],
        [(pl.BlockSpec((2, tokens, wide), lambda i: (i, 0, 0)), (width // HD, tokens, wide), BF16)],
        (lengths, queries, keys),
        40,
    )[0]


def heads_kernel(n_arrived, places, section_ref, *refs):
    probs_ref, own_refs, arrived = refs[0], refs[1:3], refs[3 : 3 + n_arrived]
    w_ref, heads_ref, mixed_ref, part_ref = refs[3 + n_arrived :]
    block = heads_ref.shape[0]
    half = own_refs[0].shape[1]
    step = pl.program_id(0)

    for section, sources in enumerate(places):

        @pl.when((step == 0) & (section_ref[0] == section))
        def _():
            for j, source in enumerate(sources):
                first_ref = own_refs[j] if source is None else arrived[source]
                mixed_ref[:, j * half : (j + 1) * half] = (
                    0.5 * own_refs[j][...].astype(F32) + 0.5 * first_ref[...].astype(F32)
                ).astype(BF16)

    first_mask, _ = head_masks(block)
    for i in range(own_refs[0].shape[0] // block):
        at = i * block
        low = max(0, at - WINDOW)

        @pl.when(step == i)
        def _():
            for pair in range(heads_ref.shape[1] // (2 * HD)):
                lanes = slice(pair * 2 * HD, (pair + 1) * 2 * HD)
                values = mixed_ref[low : at + block, lanes]
                both = [dot(probs_ref[2 * pair + h, :, : at + block - low], values) for h in range(2)]
                heads_ref[:, lanes] = jnp.where(first_mask, both[0], both[1]).astype(BF16)

    part_ref[...] = dot(heads_ref[...], w_ref[...]).astype(BF16)


def heads_proj(section, probs, own, arrived, places, w_out):
    tokens, half = own[0].shape
    width, model = w_out.shape
    n_heads, _, wide = probs.shape
    block = 256
    return call(
        lambda *refs: heads_kernel(len(arrived), places, *refs),
        (tokens // block,),
        [pl.BlockSpec(memory_space=pltpu.SMEM), pl.BlockSpec((n_heads, block, wide), lambda i: (0, i, 0))]
        + [held(tokens, half)] * (2 + len(arrived))
        + [held(width, model)],
        [
            (rows(block, width), (tokens, width), BF16),
            (whole(tokens, width), (tokens, width), BF16),
            (rows(block, model), (tokens, model), BF16),
        ],
        (section.astype(jnp.int32)[None], probs, *own, *arrived, w_out),
        40,
        name="heads",
    )


def value_back_kernel(probs_ref, attn_ref, w_ref, grad_ref, half_ref, acc):
    tokens = attn_ref.shape[0]
    block = 256
    acc[...] = jnp.zeros_like(acc)
    grad_ref[...] = dot_nt(attn_ref[...], w_ref[...]).astype(BF16)
    for at in range(0, tokens, block):
        low = max(0, at - WINDOW)
        turned_grads = grad_ref[at : at + block, :].T
        for h in range(2):
            lanes = slice(h * HD, (h + 1) * HD)
            acc[lanes, low : at + block] += dot(turned_grads[lanes], probs_ref[h, at : at + block, : at + block - low])
    for at in range(0, tokens, block):
        half_ref[at : at + block, :] = (0.5 * acc[:, at : at + block].T).astype(BF16)


def value_back(probs, grad_attn, w_out):
    tokens, model = grad_attn.shape
    width = w_out.shape[0]
    pair = columns(tokens, 2 * HD)
    return call(
        value_back_kernel,
        (width // (2 * HD),),
        [
            pl.BlockSpec((2, tokens, probs.shape[2]), lambda i: (i, 0, 0)),
            held(tokens, model),
            pl.BlockSpec((2 * HD, model), lambda i: (i, 0)),
        ],
        [(pair, (tokens, width), BF16)] * 2,
        (probs, grad_attn, w_out),
        26,
        scratch=[pltpu.VMEM((2 * HD, tokens), F32)],
    )


def attend_back_kernel(q_ref, k_ref, mixed_ref, probs_ref, grad_ref, cos_ref, sin_ref, dq_ref, dk_ref, key_acc):
    tokens = q_ref.shape[0]
    block = 256
    key_acc[...] = jnp.zeros_like(key_acc)

    def turned_back(grads, at, count):
        cos, sin = cos_ref[at : at + count, :], sin_ref[at : at + count, :]
        return (grads * cos - swap_halves(grads) * sin).astype(BF16)

    masks = head_masks(block)
    for at in range(0, tokens, block):
        low = max(0, at - WINDOW)
        grads = grad_ref[at : at + block, :]
        queries_turned = (q_ref[at : at + block, :] * BF16(HD**-0.5)).T
        keys = k_ref[low : at + block, :]
        values = mixed_ref[low : at + block, :]
        parts = []
        for h, mask in enumerate(masks):
            lanes = slice(h * HD, (h + 1) * HD)
            probs = probs_ref[h, at : at + block, : at + block - low].astype(F32)
            grad_probs = dot_nt(jnp.where(mask, grads, BF16(0)), values)
            inner = jnp.sum(probs * grad_probs, axis=1, keepdims=True)
            grad_scores = (probs * (grad_probs - inner)).astype(BF16)
            parts.append(dot(grad_scores, keys))
            key_acc[lanes, low : at + block] += dot(queries_turned[lanes], grad_scores)
        grad_query = jnp.where(masks[0], parts[0], parts[1]) * HD**-0.5
        dq_ref[at : at + block, :] = turned_back(grad_query, at, block)
    for at in range(0, tokens, block):
        dk_ref[at : at + block, :] = turned_back(key_acc[:, at : at + block].T, at, block)


def attend_back(queries, keys, mixed, probs, grad_heads, cos, sin, first, count, into):
    tokens, width = queries.shape
    pair = columns(tokens, 2 * HD, first)
    wide = probs.shape[2]
    return call(
        attend_back_kernel,
        (count,),
        [pair, pair, pair, pl.BlockSpec((2, tokens, wide), lambda i: (i + first, 0, 0)), pair]
        + [held(tokens, 128), held(tokens, 128)],
        [(pair, (tokens, width), BF16)] * 2,
        (queries, keys, mixed, probs, grad_heads, cos, sin),
        26,
        scratch=[pltpu.VMEM((2 * HD, tokens), F32)],
        into=dict(enumerate(into)),
    )


def unit_acts(normed, grad_out, w_gate, w_up, w_down, hidden_ref, dg_ref, du_ref):
    gate = dot(normed, w_gate)
    up = dot(normed, w_up)
    grad_hidden = dot_nt(grad_out, w_down)
    sig = jax.nn.sigmoid(gate)
    silu = gate * sig
    hidden = (silu * up).astype(BF16)
    hidden_ref[...] = hidden
    dg_ref[...] = (grad_hidden * up * (sig * (1.0 + gate * (1.0 - sig)))).astype(BF16)
    du_ref[...] = (grad_hidden * silu).astype(BF16)
    return hidden


def entry_kernel(n, x_ref, own_ref, other_ref, gain_ref, grad_ref, *refs):
    gates, ups, downs = (refs[j * n : (j + 1) * n] for j in range(3))
    normed_ref, hidden_ref, dg_ref, du_ref, gwd_ref, acc = refs[3 * n :]
    step = pl.program_id(0)
    middle = x_ref[...].astype(F32) + (own_ref[...].astype(F32) + other_ref[...].astype(F32))
    inv_rms = lax.rsqrt(jnp.mean(middle * middle, axis=1, keepdims=True) + EPSILON)
    normed = (middle * inv_rms * gain_ref[...]).astype(BF16)
    normed_ref[...] = normed
    w_gate, w_up = (jnp.concatenate([r[...] for r in group], axis=1) for group in (gates, ups))
    w_down = jnp.concatenate([r[...] for r in downs], axis=0)
    grad_out = grad_ref[...]
    hidden = unit_acts(normed, grad_out, w_gate, w_up, w_down, hidden_ref, dg_ref, du_ref)
    term = dot(hidden.T, grad_out)
    last = pl.num_programs(0) - 1

    @pl.when(step == 0)
    def _():
        acc[...] = term

    @pl.when((step > 0) & (step < last))
    def _():
        acc[...] += term

    @pl.when(step == last)
    def _():
        gwd_ref[...] = (acc[...] + term).astype(BF16)


def entry(x, own, other, gain, grad_out, w_gate, w_up, w_down, units):
    tokens, width = x.shape
    block = 512
    n = units // 128
    at = w_gate.shape[1] // 128 - n

    def wide(j):
        return pl.BlockSpec((width, 128), lambda i: (0, at + j), pipeline_mode=pl.Buffered(1))

    def tall(j):
        return pl.BlockSpec((128, width), lambda i: (at + j, 0), pipeline_mode=pl.Buffered(1))

    return call(
        lambda *refs: entry_kernel(n, *refs),
        (tokens // block,),
        [rows(block, width)] * 3
        + [whole(1, width), rows(block, width)]
        + [wide(j) for j in range(n)] * 2
        + [tall(j) for j in range(n)],
        [(rows(block, width), (tokens, width), BF16)]
        + [(rows(block, units), (tokens, units), BF16)] * 3
        + [(whole(units, width), (units, width), BF16)],
        (x, own, other, gain, grad_out, *[w_gate] * n, *[w_up] * n, *[w_down] * n),
        60,
        scratch=[pltpu.VMEM((units, width), F32)],
        name="entry",
    )


def ffn_kernel(normed_ref, grad_ref, wg_ref, wu_ref, wd_ref, hidden_ref, dg_ref, du_ref, gwd_ref):
    total = None
    block = normed_ref.shape[0] // 2
    for at in range(0, normed_ref.shape[0], block):
        some = pl.ds(at, block)
        grad_out = grad_ref[some, :]
        outs = (ref.at[some, :] for ref in (hidden_ref, dg_ref, du_ref))
        hidden = unit_acts(normed_ref[some, :], grad_out, wg_ref[...], wu_ref[...], wd_ref[...], *outs)
        term = dot(hidden.T, grad_out)
        total = term if total is None else total + term
    gwd_ref[...] = total.astype(BF16)


def ffn(normed, grad_out, w_gate, w_up, w_down, units, number, count, into):
    tokens, width = normed.shape
    one = pl.Buffered(1)
    return call(
        ffn_kernel,
        (1,),
        [held(tokens, width)] * 2
        + [pl.BlockSpec((width, units), lambda i: (0, number), pipeline_mode=one)] * 2
        + [pl.BlockSpec((units, width), lambda i: (number, 0), pipeline_mode=one)],
        [(columns(tokens, units, number), (tokens, units * count), BF16)] * 3
        + [(whole(units, width), (units, width), BF16)],
        (normed, grad_out, w_gate, w_up, w_down),
        40,
        into=dict(enumerate(into)),
    )


def turn_kernel(ref, out_ref):
    out_ref[...] = ref[...].T


def turned(array):
    tall, wide = array.shape
    block = 256
    return call(
        turn_kernel, (tall // block,), [rows(block, wide)], [(columns(wide, block), (wide, tall), array.dtype)], (array,), 24
    )[0]


def weight_grads_kernel(turned_ref, *refs):
    half = len(refs) // 2
    for d_ref, o_ref in zip(refs[:half], refs[half:]):
        o_ref[...] = dot(turned_ref[...], d_ref[...]).astype(BF16)


def weight_grads(left, grads, units, numbers):
    width, tokens = left.shape
    block = 512
    return call(
        weight_grads_kernel,
        (width // block,),
        [rows(block, tokens)]
        + [pl.BlockSpec((tokens, units), lambda i, at=at: (0, at), pipeline_mode=pl.Buffered(1)) for at in numbers],
        [(rows(block, units), (width, units), BF16)] * len(grads),
        (left, *grads),
        20,
    )


def row_grads_kernel(left_ref, right_ref, out_ref, left):
    @pl.when(pl.program_id(0) == 0)
    def _():
        left[...] = left_ref[...].T

    out_ref[...] = dot(left[...], right_ref[...]).astype(BF16)


def row_grads(left, right, number, tall):
    tokens, width = right.shape
    block = 512
    return call(
        row_grads_kernel,
        (width // block,),
        [pl.BlockSpec((tokens, tall), lambda i: (0, number)), columns(tokens, block)],
        [(columns(tall, block), (tall, width), BF16)],
        (left, right),
        24,
        scratch=[pltpu.VMEM((tall, tokens), BF16)],
    )[0]


def products_kernel(turn, counts, *refs):
    out_ref = refs[-1]
    n = sum(counts)
    lefts, weights = list(refs[:n]), refs[n:-1]
    total = None
    for count, w_ref in zip(counts, weights):
        at = 0
        for _ in range(count):
            left = lefts.pop(0)
            deep = left.shape[1]
            if turn:
                term = dot_nt(left[...], w_ref[:, at : at + deep])
            else:
                term = dot(left[...], w_ref[at : at + deep, :])
            at += deep
            total = term if total is None else total + term
    out_ref[...] = total.astype(BF16)


def products(pairs, turn):
    counts = [len(lefts) for lefts, _ in pairs]
    lefts = [left for group, _ in pairs for left in group]
    weights = [w for _, w in pairs]
    tokens = lefts[0].shape[0]
    width = weights[0].shape[0 if turn else 1]
    block = 256
    specs = [rows(block, w.shape[1]) if turn else columns(w.shape[0], block) for w in weights]
    return call(
        lambda *refs: products_kernel(turn, counts, *refs),
        (width // block,),
        [held(*left.shape) for left in lefts] + specs,
        [(columns(tokens, block), (tokens, width), BF16)],
        (*lefts, *weights),
        26,
        name="products",
    )[0]


def summed(refs):
    total = refs[0][...].astype(F32)
    if len(refs) > 1:
        total = total + (refs[1][...].astype(F32) + refs[2][...].astype(F32))
    return total


def norm_back_kernel(n, low, own_ref, other_ref, gain_ref, base_ref, *refs):
    values = summed(refs[:n])
    out_ref, more, gain_grad_ref = refs[n], refs[n + 1 : -1], refs[-1]
    grad_normed = own_ref[...].astype(F32) + other_ref[...].astype(F32)
    inv_rms = lax.rsqrt(jnp.mean(values * values, axis=1, keepdims=True) + EPSILON)
    weighted = grad_normed * gain_ref[...]
    inner = jnp.mean(weighted * values, axis=1, keepdims=True)
    out = base_ref[...].astype(F32) + inv_rms * weighted - values * (inv_rms * inv_rms * inv_rms) * inner
    out_ref[...] = out
    if low:
        more[0][...] = out.astype(BF16)

    @pl.when(pl.program_id(0) == 0)
    def _():
        gain_grad_ref[...] = jnp.zeros_like(gain_grad_ref)

    gain_grad_ref[...] += jnp.sum(grad_normed * values * inv_rms, axis=0, keepdims=True)


def norm_back(own, other, values, gain, base, low):
    tokens, width = own.shape
    block = 256
    outs = [(rows(block, width), (tokens, width), F32)]
    if low:
        outs.append((rows(block, width), (tokens, width), BF16))
    outs.append((whole(1, width), (1, width), F32))
    return call(
        lambda *refs: norm_back_kernel(len(values), low, *refs),
        (tokens // block,),
        [rows(block, width)] * 2 + [whole(1, width)] + [rows(block, width)] * (1 + len(values)),
        outs,
        (own, other, gain, base, *values),
        28,
        name="norm_back",
    )


def result_kernel(own_ref, other_ref, *refs):
    refs[-1][...] = (summed(refs[:-1]) + (own_ref[...].astype(F32) + other_ref[...].astype(F32))).astype(BF16)


def block_result(own, other, values):
    tokens, width = own.shape
    block = 256
    return call(
        result_kernel,
        (tokens // block,),
        [rows(block, width)] * (2 + len(values)),
        [(rows(block, width), (tokens, width), BF16)],
        (own, other, *values),
        24,
    )[0]


def sum_kernel(*refs):
    total = refs[0][...].astype(F32)
    for ref in refs[1:-1]:
        total = total + ref[...].astype(F32)
    refs[-1][...] = total.astype(BF16)


def total_of(*arrays):
    tokens, width = arrays[0].shape
    block = 512
    return call(
        sum_kernel,
        (tokens // block,),
        [rows(block, width)] * len(arrays),
        [(rows(block, width), (tokens, width), BF16)],
        arrays,
        24,
    )[0]


def first_grad_kernel(section_ref, half_ref, *refs):
    out_ref = refs[-1]

    @pl.when(section_ref[0] == 0)
    def _():
        total = half_ref[...].astype(F32)
        for ref in refs[:-1]:
            total = total + ref[...].astype(F32)
        out_ref[...] = total.astype(BF16)

    @pl.when(section_ref[0] != 0)
    def _():
        out_ref[...] = half_ref[...]


def first_grad(section, half, terms):
    tokens, width = half.shape
    block = 512
    return call(
        first_grad_kernel,
        (tokens // block,),
        [pl.BlockSpec(memory_space=pltpu.SMEM)] + [rows(block, width)] * (1 + len(terms)),
        [(rows(block, width), (tokens, width), BF16)],
        (section.astype(jnp.int32)[None], half, *terms),
        24,
    )[0]


def tie(*values):
    return lax.optimization_barrier(values)


def chosen_call(kernel, grid, flags, ins, out, shape, dtype, args, into=None):
    def spec(block, flag):
        return pl.BlockSpec(block, lambda i, j, flags: (i * flags[flag], j * flags[flag]))

    block, at = out
    kept = [] if into is None else [into]
    n = len(args)

    def body(flags_ref, *refs):
        kernel(flags_ref, *refs[:n], *refs[n + len(kept) :])

    return pl.pallas_call(
        body,
        name=kernel.__name__.removesuffix("_kernel"),
        grid_spec=pltpu.PrefetchScalarGridSpec(
            num_scalar_prefetch=1,
            grid=grid,
            in_specs=[spec(*one) for one in ins] + [pl.BlockSpec(memory_space=pl.ANY)] * len(kept),
            out_specs=pl.BlockSpec(block, lambda i, j, flags: at(i, j)),
        ),
        out_shape=jax.ShapeDtypeStruct(shape, dtype),
        input_output_aliases={1 + n: 0} if kept else {},
        compiler_params=pltpu.CompilerParams(vmem_limit_bytes=10 * MIB),
        cost_estimate=pl.CostEstimate(flops=1, bytes_accessed=1, transcendentals=0),
    )(flags, *args, *kept)


MID, END = 0, 1


def add_kernel(flags_ref, one_ref, two_ref, out_ref):
    @pl.when(flags_ref[MID] == 1)
    def _():
        out_ref[...] = (one_ref[...].astype(F32) + two_ref[...].astype(F32)).astype(BF16)


def put_kernel(flags_ref, mid_ref, end_ref, out_ref):
    @pl.when(flags_ref[MID] == 1)
    def _():
        out_ref[...] = mid_ref[...].astype(F32)

    @pl.when(flags_ref[END] == 1)
    def _():
        out_ref[...] = end_ref[...].astype(F32)


class Line:
    def __init__(self, axis, size, shapes, depth=DEPTH):
        self.axis, self.size, self.shapes, self.depth = axis, size, shapes, depth
        place = lax.axis_index(axis)
        end = (place == 0) | (place == 3)
        self.flags = jnp.stack([jnp.logical_not(end), end]).astype(jnp.int32)
        self.parts, self.places = [], []
        self.inward, self.across, self.outward, self.half, self.total = {}, {}, {}, {}, {}
        self.outs = {name: None for name in shapes}
        self.at = self.started = 0
        self.clock = []

    def after(self, *values):
        if not self.clock:
            return values if len(values) > 1 else values[0]
        tied = tie(*values, *self.clock)[: len(values)]
        return tied if len(values) > 1 else tied[0]

    def mark(self, *values):
        self.clock = list(values)

    def push(self, part, *place):
        self.parts.append(part)
        self.places.append(place)
        self.start()

    def start(self):
        while self.size == 4 and self.started < len(self.parts) and self.started < self.at + self.depth:
            i = self.started
            self.parts[i] = self.after(self.parts[i])
            self.inward[i] = lax.ppermute(self.parts[i], self.axis, [(0, 1), (3, 2)])
            self.started += 1

    def add(self, one, two):
        tall, wide = one.shape
        block = (max(tall // 2, 16), wide)
        ins = [(block, MID)] * 2
        block = (tall, wide) if tall < 32 else block
        return chosen_call(
            add_kernel, (tall // block[0], 1), self.flags, ins, (block, lambda i, j: (i, j)), one.shape, BF16, (one, two)
        )

    def step(self, drain=False):
        i, n = self.at, len(self.parts)
        if self.size != 4 or i >= n and not drain:
            return
        self.at += 1
        if i < n:
            part, arrived = self.after(self.parts[i], self.inward[i])
            self.half[i] = self.add(part, arrived)
            self.across[i] = lax.ppermute(self.half[i], self.axis, [(1, 2), (2, 1)])
            self.mark(self.half[i])
        if 0 <= i - 1 < n:
            half, arrived = self.after(self.half[i - 1], self.across[i - 1])
            self.total[i - 1] = self.add(half, arrived)
            self.outward[i - 1] = lax.ppermute(self.total[i - 1], self.axis, [(1, 0), (2, 3)])
            self.mark(self.total[i - 1])
        if 0 <= i - 2 < n:
            total, arrived = self.after(self.total[i - 2], self.outward[i - 2])
            name, block, at = self.places[i - 2]
            grid = tuple(s // b for s, b in zip(total.shape, block))
            self.outs[name] = chosen_call(
                put_kernel,
                grid,
                self.flags,
                [(block, MID), (block, END)],
                (block, at),
                self.shapes[name],
                F32,
                (total, arrived),
                self.outs[name],
            )
            self.mark(self.outs[name])
        self.start()

    def finish(self, left=0):
        if self.size == 4:
            while self.at < len(self.parts) + 2 - left:
                self.step(True)
            return
        if left:
            return
        for part, (name, block, at) in zip(self.parts, self.places):
            if self.outs[name] is None:
                self.outs[name] = jnp.zeros(self.shapes[name], F32)
            where = tuple(b * o for b, o in zip(block, at(0, 0)))
            self.outs[name] = lax.dynamic_update_slice(self.outs[name], lax.psum(part, self.axis).astype(F32), where)


def tables(lengths_row, tokens):
    seqs = lengths_row.shape[0]
    slot = jnp.arange(seqs, dtype=jnp.int32)
    ends = jnp.sum(jnp.where(slot[None, :] <= slot[:, None], lengths_row[None, :], 0), axis=1)
    places = jnp.arange(tokens, dtype=jnp.int32)
    start = jnp.sum(jnp.where(places[:, None] >= ends[None, :], lengths_row[None, :], 0), axis=1)
    position = (places - start).astype(F32)
    inv_freq = 10000.0 ** (-(jnp.arange(HD // 2, dtype=F32) * 2.0 / HD))
    angles = position[:, None] * inv_freq[None, :]
    cos, sin = jnp.cos(angles), jnp.sin(angles)
    return jnp.concatenate([cos] * 4, axis=1), jnp.concatenate([-sin, sin, -sin, sin], axis=1)


def exchange(part, axis):
    return lax.ppermute(part, axis, [(0, 1), (1, 0)])


def shards(sizes, *args):
    (x, lengths, gain_attn, w_query, w_key, w_value, w_out, gain_ffn, w_gate, w_up, w_down, grad_out) = args
    x, w_query, w_key, w_value, w_out, w_gate, w_up, w_down, grad_out = (
        a[0] for a in (x, w_query, w_key, w_value, w_out, w_gate, w_up, w_down, grad_out)
    )
    tokens, width = x.shape
    units = w_gate.shape[1]
    n_blocks = (units - 1) // UNITS
    rest = units - n_blocks * UNITS
    n_sections = sizes["section"]
    section = lax.axis_index("section")
    outputs = {"query": w_query, "key": w_key, "value": w_value, "out": w_out, "gate": w_gate, "up": w_up, "down": w_down}
    shapes = {name: w.shape for name, w in outputs.items()}
    shapes["gains"] = (16, width)
    line = Line("dp", sizes["dp"], shapes)

    def put_columns(name, first, wide):
        return name, (512, wide), lambda i, j: (i, first + j)

    def put_rows(name, first, tall):
        return name, (tall, width), lambda i, j: (first + i, 0)

    normed, *own = value_proj(x, gain_attn, w_value)

    def send(block, *pairs):
        return lax.ppermute(block, "section", list(pairs))

    relay = n_sections == 4
    if relay:
        one, two = send(own[0], (0, 1)), send(own[1], (0, 2))
    cos, sin = tables(lengths[0], tokens)
    queries, keys, turned_attn = query_key_proj(normed, w_query, w_key, cos, sin)
    if relay:
        one, two, queries = tie(one, two, queries)
        three = send(jnp.where(section == 0, own[1], one), (0, 1), (1, 3))
        four = send(jnp.where(section == 0, own[0], two), (0, 2), (2, 3))
        arrived = [one, two, three, four]
        places = [(None, None), (0, 2), (3, 1), (2, 3)]
    else:
        arrived = [send(half, (0, s)) for s in range(1, n_sections) for half in own]
        places = [(None, None)] + [(2 * s, 2 * s + 1) for s in range(n_sections - 1)]
    probs = probabilities(lengths, queries, keys)
    probs, *arrived = tie(probs, *arrived)
    heads, mixed, part = heads_proj(section, probs, own, arrived, places, w_out)
    middle = (x, part, exchange(part, "tensor"))

    weights = (w_gate, w_up, w_down)
    normed_ffn, *rest_acts, down = entry(*middle, gain_ffn, grad_out, *weights, rest)
    line.push(down, *put_rows("down", n_blocks * UNITS // 128, 128))
    line.mark(normed_ffn)
    turned_ffn = turned(line.after(normed_ffn))
    gate, up = weight_grads(turned_ffn, rest_acts[1:], rest, (0, 0))
    line.mark(gate, up)
    line.push(gate, *put_columns("gate", n_blocks * UNITS // 128, 128))
    line.push(up, *put_columns("up", n_blocks * UNITS // 128, 128))
    acts = [None] * 3
    for number in range(n_blocks):
        *acts, down = ffn(line.after(normed_ffn), grad_out, *weights, UNITS, number, n_blocks, acts)
        line.mark(down)
        line.push(down, *put_rows("down", number * UNITS // 128, 128))
        line.step()

    def unit_grads(number):
        gate, up = weight_grads(line.after(turned_ffn), acts[1:], UNITS, (number, number))
        line.mark(gate, up)
        line.push(gate, *put_columns("gate", number, UNITS))
        line.push(up, *put_columns("up", number, UNITS))

    unit_grads(0)
    line.step()
    part = products([((acts[1], line.after(rest_acts[1])), w_gate), ((acts[2], rest_acts[2]), w_up)], True)
    part_other = exchange(part, "tensor")
    line.mark(part)
    line.step()
    unit_grads(1)
    line.step()
    unit_grads(2)
    line.step()
    line.step()
    grad_middle, grad_attn, grad_gain_ffn = norm_back(line.after(part), part_other, middle, gain_ffn, grad_out, True)
    line.mark(grad_attn)
    line.step()

    grad_heads, half_mixed = value_back(probs, line.after(grad_attn), w_out)
    line.mark(grad_heads)
    if relay:
        arrived = [send(half_mixed, (1, 0), (3, 2))]
    else:
        arrived = [send(half_mixed, (s, 0)) for s in range(1, n_sections)]
    line.step()
    wide = heads.shape[1] // 2
    for number in range(2):
        part = row_grads(line.after(heads), grad_attn, number, wide)
        line.mark(part)
        line.push(part, *put_rows("out", number * wide // 128, 128))
    line.step()
    pairs = queries.shape[1] // (2 * HD)
    grads = attend_back(queries, keys, mixed, probs, line.after(grad_heads), cos, sin, 0, pairs // 2, [None] * 2)
    line.mark(*grads)
    line.step()
    terms = [half_mixed, line.after(arrived[0])] + arrived[1:]
    if relay:
        both = total_of(*terms)
        line.mark(both)
        terms = [both, send(both, (2, 0))]
    line.step()
    grad_query, grad_key = attend_back(
        queries, keys, mixed, probs, line.after(grad_heads), cos, sin, pairs // 2, pairs - pairs // 2, grads
    )
    line.mark(grad_query)

    def column_grads(name, grad):
        for number, part in enumerate(weight_grads(line.after(turned_attn), [grad] * 2, wide, (0, 1))):
            line.push(part, *put_columns(name, number, wide))
        line.mark(part)

    column_grads("query", grad_query)
    column_grads("key", grad_key)
    line.step()
    grad_value = first_grad(section, half_mixed, [line.after(terms[0])] + terms[1:])
    line.mark(grad_value)
    column_grads("value", grad_value)
    line.step()
    part = products(
        [((line.after(grad_query),), w_query), ((grad_key,), w_key), ((grad_value,), w_value)], True
    )
    part_other = exchange(part, "tensor")
    line.mark(part)
    for _ in range(GWAIT):
        line.step()
    grad_input, grad_gain_attn = norm_back(line.after(part), part_other, (x,), gain_attn, grad_middle, False)
    line.mark(grad_input)
    gains = jnp.concatenate([grad_gain_attn, grad_gain_ffn], axis=0)
    gains = jnp.pad(gains, ((0, 14), (0, 0))).astype(BF16)
    line.push(gains, "gains", (16, width), lambda i, j: (0, 0))
    line.step()
    part_result = products([((acts[0], line.after(rest_acts[0])), w_down)], False)
    line.mark(part_result)
    line.finish(LAST)
    part_result = line.after(part_result)
    result_other = exchange(part_result, "tensor")
    line.finish()
    result = block_result(part_result, line.after(result_other), middle)

    outs = line.outs
    return (
        result[None],
        grad_input[None],
        outs["gains"][0:1],
        *(outs[name][None] for name in ("query", "key", "value", "out")),
        outs["gains"][1:2],
        *(outs[name][None] for name in ("gate", "up", "down")),
    )


def solution(mesh):
    sizes = dict(mesh.shape)
    token = P("section", "dp", None)
    gain = P("section", None)
    wide, tall = P("section", None, "tensor"), P("section", "tensor", None)
    return jax.shard_map(
        lambda *args: shards(sizes, *args),
        mesh=mesh,
        in_specs=(token, P("dp", None), gain, wide, wide, wide, tall, gain, wide, wide, tall, token),
        out_specs=(token, token, gain, wide, wide, wide, tall, gain, wide, wide, tall),
        check_vma=False,
    )
```

```python
import jax
import jax.numpy as jnp
from jax import lax
from jax.experimental import pallas as pl
from jax.experimental.pallas import tpu as pltpu
from jax.sharding import PartitionSpec as P

HD = 64
WINDOW = 512
EPSILON = 1e-06
MASKED = -1e30
F32 = jnp.float32
BF16 = jnp.bfloat16
MIB = 1024 * 1024
UNITS = 384
GWAIT = 4
LAST = 2
DEPTH = 2


def dot(left, right):
    return lax.dot_general(left, right, (((1,), (0,)), ((), ())), preferred_element_type=F32)


def dot_nt(left, right):
    return lax.dot_general(left, right, (((1,), (1,)), ((), ())), preferred_element_type=F32)


def dot_tn(left, right):
    return lax.dot_general(left, right, (((0,), (0,)), ((), ())), preferred_element_type=F32)


def call(kernel, grid, ins, outs, args, vmem, scratch=(), into=None, name=None):
    into = {o: array for o, array in (into or {}).items() if array is not None}
    ins, args, n = list(ins), list(args), len(args)
    body = kernel
    if into:
        ins += [pl.BlockSpec(memory_space=pl.ANY)] * len(into)
        args += list(into.values())

        def body(*refs):
            kernel(*refs[:n], *refs[n + len(into) :])

    return pl.pallas_call(
        body,
        grid=grid,
        name=name or kernel.__name__.removesuffix("_kernel"),
        in_specs=ins,
        out_specs=[spec for spec, _, _ in outs],
        out_shape=[jax.ShapeDtypeStruct(shape, dtype) for _, shape, dtype in outs],
        scratch_shapes=list(scratch),
        input_output_aliases={n + j: o for j, o in enumerate(into)},
        compiler_params=pltpu.CompilerParams(vmem_limit_bytes=vmem * MIB),
        cost_estimate=pl.CostEstimate(flops=1, bytes_accessed=1, transcendentals=0),
    )(*args)


def rows(block, width):
    return pl.BlockSpec((block, width), lambda i: (i, 0))


def whole(*shape):
    return pl.BlockSpec(shape, lambda i: (0,) * len(shape))


def held(*shape):
    return pl.BlockSpec(shape, lambda i: (0,) * len(shape), pipeline_mode=pl.Buffered(1))


def columns(height, block, first=0):
    return pl.BlockSpec((height, block), lambda i: (0, i + first))


def value_kernel(x_ref, gain_ref, w_ref, normed_ref, *value_refs):
    x = x_ref[...].astype(F32)
    inv_rms = lax.rsqrt(jnp.mean(x * x, axis=1, keepdims=True) + EPSILON)
    normed = (x * inv_rms * gain_ref[...]).astype(BF16)
    normed_ref[...] = normed
    values = dot(normed, w_ref[...]).astype(BF16)
    cut = values.shape[1] // len(value_refs)
    for j, ref in enumerate(value_refs):
        ref[...] = values[:, j * cut : (j + 1) * cut]


def value_proj(x, gain, w_value):
    tokens, width = x.shape
    half = w_value.shape[1] // 2
    block = 256
    return call(
        value_kernel,
        (tokens // block,),
        [rows(block, width), held(1, width), held(width, 2 * half)],
        [(rows(block, width), (tokens, width), BF16)] + [(rows(block, half), (tokens, half), BF16)] * 2,
        (x, gain, w_value),
        60,
    )


def swap_halves(u):
    lane = lax.broadcasted_iota(jnp.int32, u.shape, 1) % HD
    return jnp.where(lane < HD // 2, pltpu.roll(u, 128 - HD // 2, 1), pltpu.roll(u, HD // 2, 1))


def query_key_kernel(n_ref, wq_ref, wk_ref, cos_ref, sin_ref, q_ref, k_ref, turned_ref):
    normed = n_ref[...]
    cos, sin = cos_ref[...], sin_ref[...]
    for w_ref, o_ref in ((wq_ref, q_ref), (wk_ref, k_ref)):
        u = dot(normed, w_ref[...])
        for lo in range(0, u.shape[1], 128):
            part = u[:, lo : lo + 128]
            o_ref[:, lo : lo + 128] = (part * cos + swap_halves(part) * sin).astype(BF16)
    turned_ref[...] = normed.T


def query_key_proj(normed, w_query, w_key, cos, sin):
    tokens, width = normed.shape
    out = w_query.shape[1]
    block = 256
    return call(
        query_key_kernel,
        (tokens // block,),
        [rows(block, width), held(width, out), held(width, out), rows(block, 128), rows(block, 128)],
        [
            (rows(block, out), (tokens, out), BF16),
            (rows(block, out), (tokens, out), BF16),
            (columns(width, block), (width, tokens), BF16),
        ],
        (normed, w_query, w_key, cos, sin),
        32,
    )


def row_starts(len_ref, first, count):
    place = first + lax.broadcasted_iota(jnp.int32, (count, 1), 0)
    start = jnp.zeros((count, 1), jnp.int32)
    end = 0
    for j in range(len_ref.shape[1]):
        end = end + len_ref[0, j]
        start = jnp.where(place >= end, end, start)
    return place, start


def band(len_ref, first, count):
    low = max(0, first - WINDOW)
    place, start = row_starts(len_ref, first, count)
    col = low + lax.broadcasted_iota(jnp.int32, (count, first + count - low), 1)
    return low, (col >= start) & (col <= place)


def head_masks(count):
    lane = lax.broadcasted_iota(jnp.int32, (count, 2 * HD), 1)
    return lane < HD, lane >= HD


def probs_kernel(len_ref, q_ref, k_ref, probs_ref):
    tokens = q_ref.shape[0]
    block = 256
    for at in range(0, tokens, block):
        low, allowed = band(len_ref, at, block)
        queries = q_ref[at : at + block, :] * BF16(HD**-0.5)
        keys = k_ref[low : at + block, :]
        for h, mask in enumerate(head_masks(block)):
            scores = dot_nt(jnp.where(mask, queries, BF16(0)), keys)
            scores = jnp.where(allowed, scores, MASKED)
            exps = jnp.exp(scores - jnp.max(scores, axis=1, keepdims=True))
            total = jnp.sum(exps, axis=1, keepdims=True)
            probs_ref[h, at : at + block, : at + block - low] = (exps * (1.0 / total)).astype(BF16)


def band_width(tokens):
    return min(tokens, WINDOW + 256)


def probabilities(lengths, queries, keys):
    tokens, width = queries.shape
    pair = columns(tokens, 2 * HD)
    wide = band_width(tokens)
    return call(
        probs_kernel,
        (width // (2 * HD),),
        [pl.BlockSpec(memory_space=pltpu.SMEM), pair, pair],
        [(pl.BlockSpec((2, tokens, wide), lambda i: (i, 0, 0)), (width // HD, tokens, wide), BF16)],
        (lengths, queries, keys),
        40,
    )[0]


def heads_kernel(n_arrived, places, section_ref, *refs):
    probs_ref, own_refs, arrived = refs[0], refs[1:3], refs[3 : 3 + n_arrived]
    w_ref, heads_ref, mixed_ref, part_ref = refs[3 + n_arrived :]
    block = heads_ref.shape[0]
    half = own_refs[0].shape[1]
    step = pl.program_id(0)

    for section, sources in enumerate(places):

        @pl.when((step == 0) & (section_ref[0] == section))
        def _():
            for j, source in enumerate(sources):
                first_ref = own_refs[j] if source is None else arrived[source]
                mixed_ref[:, j * half : (j + 1) * half] = (
                    0.5 * own_refs[j][...].astype(F32) + 0.5 * first_ref[...].astype(F32)
                ).astype(BF16)

    first_mask, _ = head_masks(block)
    for i in range(own_refs[0].shape[0] // block):
        at = i * block
        low = max(0, at - WINDOW)

        @pl.when(step == i)
        def _():
            for pair in range(heads_ref.shape[1] // (2 * HD)):
                lanes = slice(pair * 2 * HD, (pair + 1) * 2 * HD)
                values = mixed_ref[low : at + block, lanes]
                both = [dot(probs_ref[2 * pair + h, :, : at + block - low], values) for h in range(2)]
                heads_ref[:, lanes] = jnp.where(first_mask, both[0], both[1]).astype(BF16)

    part_ref[...] = dot(heads_ref[...], w_ref[...]).astype(BF16)


def heads_proj(section, probs, own, arrived, places, w_out):
    tokens, half = own[0].shape
    width, model = w_out.shape
    n_heads, _, wide = probs.shape
    block = 256
    return call(
        lambda *refs: heads_kernel(len(arrived), places, *refs),
        (tokens // block,),
        [pl.BlockSpec(memory_space=pltpu.SMEM), pl.BlockSpec((n_heads, block, wide), lambda i: (0, i, 0))]
        + [held(tokens, half)] * (2 + len(arrived))
        + [held(width, model)],
        [
            (rows(block, width), (tokens, width), BF16),
            (whole(tokens, width), (tokens, width), BF16),
            (rows(block, model), (tokens, model), BF16),
        ],
        (section.astype(jnp.int32)[None], probs, *own, *arrived, w_out),
        40,
        name="heads",
    )


def value_back_kernel(probs_ref, attn_ref, w_ref, grad_ref, half_ref, acc):
    tokens = attn_ref.shape[0]
    block = 256
    acc[...] = jnp.zeros_like(acc)
    grad_ref[...] = dot_nt(attn_ref[...], w_ref[...]).astype(BF16)
    for at in range(0, tokens, block):
        low = max(0, at - WINDOW)
        turned_grads = grad_ref[at : at + block, :].T
        for h in range(2):
            lanes = slice(h * HD, (h + 1) * HD)
            acc[lanes, low : at + block] += dot(turned_grads[lanes], probs_ref[h, at : at + block, : at + block - low])
    for at in range(0, tokens, block):
        half_ref[at : at + block, :] = (0.5 * acc[:, at : at + block].T).astype(BF16)


def value_back(probs, grad_attn, w_out):
    tokens, model = grad_attn.shape
    width = w_out.shape[0]
    pair = columns(tokens, 2 * HD)
    return call(
        value_back_kernel,
        (width // (2 * HD),),
        [
            pl.BlockSpec((2, tokens, probs.shape[2]), lambda i: (i, 0, 0)),
            held(tokens, model),
            pl.BlockSpec((2 * HD, model), lambda i: (i, 0)),
        ],
        [(pair, (tokens, width), BF16)] * 2,
        (probs, grad_attn, w_out),
        26,
        scratch=[pltpu.VMEM((2 * HD, tokens), F32)],
    )


def attend_back_kernel(q_ref, k_ref, mixed_ref, probs_ref, grad_ref, cos_ref, sin_ref, dq_ref, dk_ref, key_acc):
    tokens = q_ref.shape[0]
    block = 256
    key_acc[...] = jnp.zeros_like(key_acc)

    def turned_back(grads, at, count):
        cos, sin = cos_ref[at : at + count, :], sin_ref[at : at + count, :]
        return (grads * cos - swap_halves(grads) * sin).astype(BF16)

    masks = head_masks(block)
    for at in range(0, tokens, block):
        low = max(0, at - WINDOW)
        grads = grad_ref[at : at + block, :]
        queries_turned = (q_ref[at : at + block, :] * BF16(HD**-0.5)).T
        keys = k_ref[low : at + block, :]
        values = mixed_ref[low : at + block, :]
        parts = []
        for h, mask in enumerate(masks):
            lanes = slice(h * HD, (h + 1) * HD)
            probs = probs_ref[h, at : at + block, : at + block - low].astype(F32)
            grad_probs = dot_nt(jnp.where(mask, grads, BF16(0)), values)
            inner = jnp.sum(probs * grad_probs, axis=1, keepdims=True)
            grad_scores = (probs * (grad_probs - inner)).astype(BF16)
            parts.append(dot(grad_scores, keys))
            key_acc[lanes, low : at + block] += dot(queries_turned[lanes], grad_scores)
        grad_query = jnp.where(masks[0], parts[0], parts[1]) * HD**-0.5
        dq_ref[at : at + block, :] = turned_back(grad_query, at, block)
    for at in range(0, tokens, block):
        dk_ref[at : at + block, :] = turned_back(key_acc[:, at : at + block].T, at, block)


def attend_back(queries, keys, mixed, probs, grad_heads, cos, sin, first, count, into):
    tokens, width = queries.shape
    pair = columns(tokens, 2 * HD, first)
    wide = probs.shape[2]
    return call(
        attend_back_kernel,
        (count,),
        [pair, pair, pair, pl.BlockSpec((2, tokens, wide), lambda i: (i + first, 0, 0)), pair]
        + [held(tokens, 128), held(tokens, 128)],
        [(pair, (tokens, width), BF16)] * 2,
        (queries, keys, mixed, probs, grad_heads, cos, sin),
        26,
        scratch=[pltpu.VMEM((2 * HD, tokens), F32)],
        into=dict(enumerate(into)),
    )


def unit_acts(normed, grad_out, w_gate, w_up, w_down, hidden_ref, dg_ref, du_ref):
    gate = dot(normed, w_gate)
    up = dot(normed, w_up)
    grad_hidden = dot_nt(grad_out, w_down)
    sig = jax.nn.sigmoid(gate)
    silu = gate * sig
    hidden = (silu * up).astype(BF16)
    hidden_ref[...] = hidden
    dg_ref[...] = (grad_hidden * up * (sig * (1.0 + gate * (1.0 - sig)))).astype(BF16)
    du_ref[...] = (grad_hidden * silu).astype(BF16)
    return hidden


def entry_kernel(n, x_ref, own_ref, other_ref, gain_ref, grad_ref, *refs):
    gates, ups, downs = (refs[j * n : (j + 1) * n] for j in range(3))
    normed_ref, hidden_ref, dg_ref, du_ref, gwd_ref, acc = refs[3 * n :]
    step = pl.program_id(0)
    middle = x_ref[...].astype(F32) + (own_ref[...].astype(F32) + other_ref[...].astype(F32))
    inv_rms = lax.rsqrt(jnp.mean(middle * middle, axis=1, keepdims=True) + EPSILON)
    normed = (middle * inv_rms * gain_ref[...]).astype(BF16)
    normed_ref[...] = normed
    w_gate, w_up = (jnp.concatenate([r[...] for r in group], axis=1) for group in (gates, ups))
    w_down = jnp.concatenate([r[...] for r in downs], axis=0)
    grad_out = grad_ref[...]
    hidden = unit_acts(normed, grad_out, w_gate, w_up, w_down, hidden_ref, dg_ref, du_ref)
    term = dot(hidden.T, grad_out)
    last = pl.num_programs(0) - 1

    @pl.when(step == 0)
    def _():
        acc[...] = term

    @pl.when((step > 0) & (step < last))
    def _():
        acc[...] += term

    @pl.when(step == last)
    def _():
        gwd_ref[...] = (acc[...] + term).astype(BF16)


def entry(x, own, other, gain, grad_out, w_gate, w_up, w_down, units):
    tokens, width = x.shape
    block = 512
    n = units // 128
    at = w_gate.shape[1] // 128 - n

    def wide(j):
        return pl.BlockSpec((width, 128), lambda i: (0, at + j), pipeline_mode=pl.Buffered(1))

    def tall(j):
        return pl.BlockSpec((128, width), lambda i: (at + j, 0), pipeline_mode=pl.Buffered(1))

    return call(
        lambda *refs: entry_kernel(n, *refs),
        (tokens // block,),
        [rows(block, width)] * 3
        + [whole(1, width), rows(block, width)]
        + [wide(j) for j in range(n)] * 2
        + [tall(j) for j in range(n)],
        [(rows(block, width), (tokens, width), BF16)]
        + [(rows(block, units), (tokens, units), BF16)] * 3
        + [(whole(units, width), (units, width), BF16)],
        (x, own, other, gain, grad_out, *[w_gate] * n, *[w_up] * n, *[w_down] * n),
        60,
        scratch=[pltpu.VMEM((units, width), F32)],
        name="entry",
    )


def ffn_kernel(normed_ref, grad_ref, wg_ref, wu_ref, wd_ref, hidden_ref, dg_ref, du_ref, gwd_ref):
    total = None
    block = normed_ref.shape[0] // 2
    for at in range(0, normed_ref.shape[0], block):
        some = pl.ds(at, block)
        grad_out = grad_ref[some, :]
        outs = (ref.at[some, :] for ref in (hidden_ref, dg_ref, du_ref))
        hidden = unit_acts(normed_ref[some, :], grad_out, wg_ref[...], wu_ref[...], wd_ref[...], *outs)
        term = dot(hidden.T, grad_out)
        total = term if total is None else total + term
    gwd_ref[...] = total.astype(BF16)


def ffn(normed, grad_out, w_gate, w_up, w_down, units, number, count, into):
    tokens, width = normed.shape
    one = pl.Buffered(1)
    return call(
        ffn_kernel,
        (1,),
        [held(tokens, width)] * 2
        + [pl.BlockSpec((width, units), lambda i: (0, number), pipeline_mode=one)] * 2
        + [pl.BlockSpec((units, width), lambda i: (number, 0), pipeline_mode=one)],
        [(columns(tokens, units, number), (tokens, units * count), BF16)] * 3
        + [(whole(units, width), (units, width), BF16)],
        (normed, grad_out, w_gate, w_up, w_down),
        40,
        into=dict(enumerate(into)),
    )


def turn_kernel(ref, out_ref):
    out_ref[...] = ref[...].T


def turned(array):
    tall, wide = array.shape
    block = 256
    return call(
        turn_kernel, (tall // block,), [rows(block, wide)], [(columns(wide, block), (wide, tall), array.dtype)], (array,), 24
    )[0]


def weight_grads_kernel(turned_ref, *refs):
    half = len(refs) // 2
    for d_ref, o_ref in zip(refs[:half], refs[half:]):
        o_ref[...] = dot(turned_ref[...], d_ref[...]).astype(BF16)


def weight_grads(left, grads, units, numbers):
    width, tokens = left.shape
    block = 512
    return call(
        weight_grads_kernel,
        (width // block,),
        [rows(block, tokens)]
        + [pl.BlockSpec((tokens, units), lambda i, at=at: (0, at), pipeline_mode=pl.Buffered(1)) for at in numbers],
        [(rows(block, units), (width, units), BF16)] * len(grads),
        (left, *grads),
        20,
    )


def row_grads_kernel(left_ref, right_ref, out_ref, left):
    @pl.when(pl.program_id(0) == 0)
    def _():
        left[...] = left_ref[...].T

    out_ref[...] = dot(left[...], right_ref[...]).astype(BF16)


def row_grads(left, right, number, tall):
    tokens, width = right.shape
    block = 512
    return call(
        row_grads_kernel,
        (width // block,),
        [pl.BlockSpec((tokens, tall), lambda i: (0, number)), columns(tokens, block)],
        [(columns(tall, block), (tall, width), BF16)],
        (left, right),
        24,
        scratch=[pltpu.VMEM((tall, tokens), BF16)],
    )[0]


def products_kernel(turn, counts, *refs):
    out_ref = refs[-1]
    n = sum(counts)
    lefts, weights = list(refs[:n]), refs[n:-1]
    total = None
    for count, w_ref in zip(counts, weights):
        at = 0
        for _ in range(count):
            left = lefts.pop(0)
            deep = left.shape[1]
            if turn:
                term = dot_nt(left[...], w_ref[:, at : at + deep])
            else:
                term = dot(left[...], w_ref[at : at + deep, :])
            at += deep
            total = term if total is None else total + term
    out_ref[...] = total.astype(BF16)


def products(pairs, turn):
    counts = [len(lefts) for lefts, _ in pairs]
    lefts = [left for group, _ in pairs for left in group]
    weights = [w for _, w in pairs]
    tokens = lefts[0].shape[0]
    width = weights[0].shape[0 if turn else 1]
    block = 256
    specs = [rows(block, w.shape[1]) if turn else columns(w.shape[0], block) for w in weights]
    return call(
        lambda *refs: products_kernel(turn, counts, *refs),
        (width // block,),
        [held(*left.shape) for left in lefts] + specs,
        [(columns(tokens, block), (tokens, width), BF16)],
        (*lefts, *weights),
        26,
        name="products",
    )[0]


def summed(refs):
    total = refs[0][...].astype(F32)
    if len(refs) > 1:
        total = total + (refs[1][...].astype(F32) + refs[2][...].astype(F32))
    return total


def norm_back_kernel(n, low, own_ref, other_ref, gain_ref, base_ref, *refs):
    values = summed(refs[:n])
    out_ref, more, gain_grad_ref = refs[n], refs[n + 1 : -1], refs[-1]
    grad_normed = own_ref[...].astype(F32) + other_ref[...].astype(F32)
    inv_rms = lax.rsqrt(jnp.mean(values * values, axis=1, keepdims=True) + EPSILON)
    weighted = grad_normed * gain_ref[...]
    inner = jnp.mean(weighted * values, axis=1, keepdims=True)
    out = base_ref[...].astype(F32) + inv_rms * weighted - values * (inv_rms * inv_rms * inv_rms) * inner
    out_ref[...] = out
    if low:
        more[0][...] = out.astype(BF16)

    @pl.when(pl.program_id(0) == 0)
    def _():
        gain_grad_ref[...] = jnp.zeros_like(gain_grad_ref)

    gain_grad_ref[...] += jnp.sum(grad_normed * values * inv_rms, axis=0, keepdims=True)


def norm_back(own, other, values, gain, base, low):
    tokens, width = own.shape
    block = 256
    outs = [(rows(block, width), (tokens, width), F32)]
    if low:
        outs.append((rows(block, width), (tokens, width), BF16))
    outs.append((whole(1, width), (1, width), F32))
    return call(
        lambda *refs: norm_back_kernel(len(values), low, *refs),
        (tokens // block,),
        [rows(block, width)] * 2 + [whole(1, width)] + [rows(block, width)] * (1 + len(values)),
        outs,
        (own, other, gain, base, *values),
        28,
        name="norm_back",
    )


def result_kernel(own_ref, other_ref, *refs):
    refs[-1][...] = (summed(refs[:-1]) + (own_ref[...].astype(F32) + other_ref[...].astype(F32))).astype(BF16)


def block_result(own, other, values):
    tokens, width = own.shape
    block = 256
    return call(
        result_kernel,
        (tokens // block,),
        [rows(block, width)] * (2 + len(values)),
        [(rows(block, width), (tokens, width), BF16)],
        (own, other, *values),
        24,
    )[0]


def sum_kernel(*refs):
    total = refs[0][...].astype(F32)
    for ref in refs[1:-1]:
        total = total + ref[...].astype(F32)
    refs[-1][...] = total.astype(BF16)


def total_of(*arrays):
    tokens, width = arrays[0].shape
    block = 512
    return call(
        sum_kernel,
        (tokens // block,),
        [rows(block, width)] * len(arrays),
        [(rows(block, width), (tokens, width), BF16)],
        arrays,
        24,
    )[0]


def first_grad_kernel(section_ref, half_ref, *refs):
    out_ref = refs[-1]

    @pl.when(section_ref[0] == 0)
    def _():
        total = half_ref[...].astype(F32)
        for ref in refs[:-1]:
            total = total + ref[...].astype(F32)
        out_ref[...] = total.astype(BF16)

    @pl.when(section_ref[0] != 0)
    def _():
        out_ref[...] = half_ref[...]


def first_grad(section, half, terms):
    tokens, width = half.shape
    block = 512
    return call(
        first_grad_kernel,
        (tokens // block,),
        [pl.BlockSpec(memory_space=pltpu.SMEM)] + [rows(block, width)] * (1 + len(terms)),
        [(rows(block, width), (tokens, width), BF16)],
        (section.astype(jnp.int32)[None], half, *terms),
        24,
    )[0]


def tie(*values):
    return lax.optimization_barrier(values)


def chosen_call(kernel, grid, flags, ins, out, shape, dtype, args, into=None):
    def spec(block, flag):
        return pl.BlockSpec(block, lambda i, j, flags: (i * flags[flag], j * flags[flag]))

    block, at = out
    kept = [] if into is None else [into]
    n = len(args)

    def body(flags_ref, *refs):
        kernel(flags_ref, *refs[:n], *refs[n + len(kept) :])

    return pl.pallas_call(
        body,
        name=kernel.__name__.removesuffix("_kernel"),
        grid_spec=pltpu.PrefetchScalarGridSpec(
            num_scalar_prefetch=1,
            grid=grid,
            in_specs=[spec(*one) for one in ins] + [pl.BlockSpec(memory_space=pl.ANY)] * len(kept),
            out_specs=pl.BlockSpec(block, lambda i, j, flags: at(i, j)),
        ),
        out_shape=jax.ShapeDtypeStruct(shape, dtype),
        input_output_aliases={1 + n: 0} if kept else {},
        compiler_params=pltpu.CompilerParams(vmem_limit_bytes=10 * MIB),
        cost_estimate=pl.CostEstimate(flops=1, bytes_accessed=1, transcendentals=0),
    )(flags, *args, *kept)


MID, END = 0, 1


def add_kernel(flags_ref, one_ref, two_ref, out_ref):
    @pl.when(flags_ref[MID] == 1)
    def _():
        out_ref[...] = (one_ref[...].astype(F32) + two_ref[...].astype(F32)).astype(BF16)


def put_kernel(flags_ref, mid_ref, end_ref, out_ref):
    @pl.when(flags_ref[MID] == 1)
    def _():
        out_ref[...] = mid_ref[...].astype(F32)

    @pl.when(flags_ref[END] == 1)
    def _():
        out_ref[...] = end_ref[...].astype(F32)


class Line:
    def __init__(self, axis, size, shapes, depth=DEPTH):
        self.axis, self.size, self.shapes, self.depth = axis, size, shapes, depth
        place = lax.axis_index(axis)
        end = (place == 0) | (place == 3)
        self.flags = jnp.stack([jnp.logical_not(end), end]).astype(jnp.int32)
        self.parts, self.places = [], []
        self.inward, self.across, self.outward, self.half, self.total = {}, {}, {}, {}, {}
        self.outs = {name: None for name in shapes}
        self.at = self.started = 0
        self.clock = []

    def after(self, *values):
        if not self.clock:
            return values if len(values) > 1 else values[0]
        tied = tie(*values, *self.clock)[: len(values)]
        return tied if len(values) > 1 else tied[0]

    def mark(self, *values):
        self.clock = list(values)

    def push(self, part, *place):
        self.parts.append(part)
        self.places.append(place)
        self.start()

    def start(self):
        while self.size == 4 and self.started < len(self.parts) and self.started < self.at + self.depth:
            i = self.started
            self.parts[i] = self.after(self.parts[i])
            self.inward[i] = lax.ppermute(self.parts[i], self.axis, [(0, 1), (3, 2)])
            self.started += 1

    def add(self, one, two):
        tall, wide = one.shape
        block = (max(tall // 2, 16), wide)
        ins = [(block, MID)] * 2
        block = (tall, wide) if tall < 32 else block
        return chosen_call(
            add_kernel, (tall // block[0], 1), self.flags, ins, (block, lambda i, j: (i, j)), one.shape, BF16, (one, two)
        )

    def step(self, drain=False):
        i, n = self.at, len(self.parts)
        if self.size != 4 or i >= n and not drain:
            return
        self.at += 1
        if i < n:
            part, arrived = self.after(self.parts[i], self.inward[i])
            self.half[i] = self.add(part, arrived)
            self.across[i] = lax.ppermute(self.half[i], self.axis, [(1, 2), (2, 1)])
            self.mark(self.half[i])
        if 0 <= i - 1 < n:
            half, arrived = self.after(self.half[i - 1], self.across[i - 1])
            self.total[i - 1] = self.add(half, arrived)
            self.outward[i - 1] = lax.ppermute(self.total[i - 1], self.axis, [(1, 0), (2, 3)])
            self.mark(self.total[i - 1])
        if 0 <= i - 2 < n:
            total, arrived = self.after(self.total[i - 2], self.outward[i - 2])
            name, block, at = self.places[i - 2]
            grid = tuple(s // b for s, b in zip(total.shape, block))
            self.outs[name] = chosen_call(
                put_kernel,
                grid,
                self.flags,
                [(block, MID), (block, END)],
                (block, at),
                self.shapes[name],
                F32,
                (total, arrived),
                self.outs[name],
            )
            self.mark(self.outs[name])
        self.start()

    def finish(self, left=0):
        if self.size == 4:
            while self.at < len(self.parts) + 2 - left:
                self.step(True)
            return
        if left:
            return
        for part, (name, block, at) in zip(self.parts, self.places):
            if self.outs[name] is None:
                self.outs[name] = jnp.zeros(self.shapes[name], F32)
            where = tuple(b * o for b, o in zip(block, at(0, 0)))
            self.outs[name] = lax.dynamic_update_slice(self.outs[name], lax.psum(part, self.axis).astype(F32), where)


def tables(lengths_row, tokens):
    seqs = lengths_row.shape[0]
    slot = jnp.arange(seqs, dtype=jnp.int32)
    ends = jnp.sum(jnp.where(slot[None, :] <= slot[:, None], lengths_row[None, :], 0), axis=1)
    places = jnp.arange(tokens, dtype=jnp.int32)
    start = jnp.sum(jnp.where(places[:, None] >= ends[None, :], lengths_row[None, :], 0), axis=1)
    position = (places - start).astype(F32)
    inv_freq = 10000.0 ** (-(jnp.arange(HD // 2, dtype=F32) * 2.0 / HD))
    angles = position[:, None] * inv_freq[None, :]
    cos, sin = jnp.cos(angles), jnp.sin(angles)
    return jnp.concatenate([cos] * 4, axis=1), jnp.concatenate([-sin, sin, -sin, sin], axis=1)


def exchange(part, axis):
    return lax.ppermute(part, axis, [(0, 1), (1, 0)])


def shards(sizes, *args):
    (x, lengths, gain_attn, w_query, w_key, w_value, w_out, gain_ffn, w_gate, w_up, w_down, grad_out) = args
    x, w_query, w_key, w_value, w_out, w_gate, w_up, w_down, grad_out = (
        a[0] for a in (x, w_query, w_key, w_value, w_out, w_gate, w_up, w_down, grad_out)
    )
    tokens, width = x.shape
    units = w_gate.shape[1]
    n_blocks = (units - 1) // UNITS
    rest = units - n_blocks * UNITS
    n_sections = sizes["section"]
    section = lax.axis_index("section")
    outputs = {"query": w_query, "key": w_key, "value": w_value, "out": w_out, "gate": w_gate, "up": w_up, "down": w_down}
    shapes = {name: w.shape for name, w in outputs.items()}
    shapes["gains"] = (16, width)
    line = Line("dp", sizes["dp"], shapes)

    def put_columns(name, first, wide):
        return name, (512, wide), lambda i, j: (i, first + j)

    def put_rows(name, first, tall):
        return name, (tall, width), lambda i, j: (first + i, 0)

    normed, *own = value_proj(x, gain_attn, w_value)

    def send(block, *pairs):
        return lax.ppermute(block, "section", list(pairs))

    relay = n_sections == 4
    if relay:
        one, two = send(own[0], (0, 1)), send(own[1], (0, 2))
    cos, sin = tables(lengths[0], tokens)
    queries, keys, turned_attn = query_key_proj(normed, w_query, w_key, cos, sin)
    if relay:
        one, two, queries = tie(one, two, queries)
        three = send(jnp.where(section == 0, own[1], one), (0, 1), (1, 3))
        four = send(jnp.where(section == 0, own[0], two), (0, 2), (2, 3))
        arrived = [one, two, three, four]
        places = [(None, None), (0, 2), (3, 1), (2, 3)]
    else:
        arrived = [send(half, (0, s)) for s in range(1, n_sections) for half in own]
        places = [(None, None)] + [(2 * s, 2 * s + 1) for s in range(n_sections - 1)]
    probs = probabilities(lengths, queries, keys)
    probs, *arrived = tie(probs, *arrived)
    heads, mixed, part = heads_proj(section, probs, own, arrived, places, w_out)
    middle = (x, part, exchange(part, "tensor"))

    weights = (w_gate, w_up, w_down)
    normed_ffn, *rest_acts, down = entry(*middle, gain_ffn, grad_out, *weights, rest)
    line.push(down, *put_rows("down", n_blocks * UNITS // 128, 128))
    line.mark(normed_ffn)
    turned_ffn = turned(line.after(normed_ffn))
    gate, up = weight_grads(turned_ffn, rest_acts[1:], rest, (0, 0))
    line.mark(gate, up)
    line.push(gate, *put_columns("gate", n_blocks * UNITS // 128, 128))
    line.push(up, *put_columns("up", n_blocks * UNITS // 128, 128))
    acts = [None] * 3
    for number in range(n_blocks):
        *acts, down = ffn(line.after(normed_ffn), grad_out, *weights, UNITS, number, n_blocks, acts)
        line.mark(down)
        line.push(down, *put_rows("down", number * UNITS // 128, 128))
        line.step()

    def unit_grads(number):
        gate, up = weight_grads(line.after(turned_ffn), acts[1:], UNITS, (number, number))
        line.mark(gate, up)
        line.push(gate, *put_columns("gate", number, UNITS))
        line.push(up, *put_columns("up", number, UNITS))

    unit_grads(0)
    line.step()
    line.depth = 3
    part = products([((acts[1], line.after(rest_acts[1])), w_gate), ((acts[2], rest_acts[2]), w_up)], True)
    part_other = exchange(part, "tensor")
    line.mark(part)
    line.step()
    unit_grads(1)
    line.step()
    unit_grads(2)
    line.step()
    line.step()
    grad_middle, grad_attn, grad_gain_ffn = norm_back(line.after(part), part_other, middle, gain_ffn, grad_out, True)
    line.mark(grad_attn)
    line.step()

    grad_heads, half_mixed = value_back(probs, line.after(grad_attn), w_out)
    line.mark(grad_heads)
    if relay:
        arrived = [send(half_mixed, (1, 0), (3, 2))]
    else:
        arrived = [send(half_mixed, (s, 0)) for s in range(1, n_sections)]
    line.step()
    wide = heads.shape[1] // 2
    pairs = queries.shape[1] // (2 * HD)
    grads = [None] * 2

    def some_pairs(first, count):
        out = attend_back(queries, keys, mixed, probs, line.after(grad_heads), cos, sin, first, count, grads)
        line.mark(*out)
        return out

    for number in range(2):
        part = row_grads(line.after(heads), grad_attn, number, wide)
        line.mark(part)
        line.push(part, *put_rows("out", number * wide // 128, 128))
    cuts = [pairs * j // 4 for j in range(5)]
    grads = some_pairs(cuts[0], cuts[1] - cuts[0])
    line.step()
    grads = some_pairs(cuts[1], cuts[2] - cuts[1])
    line.step()
    terms = [half_mixed, line.after(arrived[0])] + arrived[1:]
    if relay:
        both = total_of(*terms)
        line.mark(both)
        terms = [both, send(both, (2, 0))]
    grads = some_pairs(cuts[2], cuts[3] - cuts[2])
    line.step()
    grads = some_pairs(cuts[3], cuts[4] - cuts[3])
    grad_query, grad_key = grads

    def column_grads(name, grad):
        for number, part in enumerate(weight_grads(line.after(turned_attn), [grad] * 2, wide, (0, 1))):
            line.push(part, *put_columns(name, number, wide))
        line.mark(part)

    column_grads("query", grad_query)
    column_grads("key", grad_key)
    line.step()
    grad_value = first_grad(section, half_mixed, [line.after(terms[0])] + terms[1:])
    line.mark(grad_value)
    column_grads("value", grad_value)
    line.step()
    part = products(
        [((line.after(grad_query),), w_query), ((grad_key,), w_key), ((grad_value,), w_value)], True
    )
    part_other = exchange(part, "tensor")
    line.mark(part)
    for _ in range(GWAIT):
        line.step()
    grad_input, grad_gain_attn = norm_back(line.after(part), part_other, (x,), gain_attn, grad_middle, False)
    line.mark(grad_input)
    gains = jnp.concatenate([grad_gain_attn, grad_gain_ffn], axis=0)
    gains = jnp.pad(gains, ((0, 14), (0, 0))).astype(BF16)
    line.push(gains, "gains", (16, width), lambda i, j: (0, 0))
    line.step()
    part_result = products([((acts[0], line.after(rest_acts[0])), w_down)], False)
    line.mark(part_result)
    line.finish(LAST)
    part_result = line.after(part_result)
    result_other = exchange(part_result, "tensor")
    line.finish()
    result = block_result(part_result, line.after(result_other), middle)

    outs = line.outs
    return (
        result[None],
        grad_input[None],
        outs["gains"][0:1],
        *(outs[name][None] for name in ("query", "key", "value", "out")),
        outs["gains"][1:2],
        *(outs[name][None] for name in ("gate", "up", "down")),
    )


def solution(mesh):
    sizes = dict(mesh.shape)
    token = P("section", "dp", None)
    gain = P("section", None)
    wide, tall = P("section", None, "tensor"), P("section", "tensor", None)
    return jax.shard_map(
        lambda *args: shards(sizes, *args),
        mesh=mesh,
        in_specs=(token, P("dp", None), gain, wide, wide, wide, tall, gain, wide, wide, tall, token),
        out_specs=(token, token, gain, wide, wide, wide, tall, gain, wide, wide, tall),
        check_vma=False,
    )
```
